32 devices in a mesh: tiles: 32 (over z, y, x, core).
Axes of the slice: x: 2, y: 2, z: 4, core: 2. Of those that a mesh axis runs over, the one named last changes fastest.
Arguments:
- primal_start: float32 [64, 512, 1024], P('tiles'), may hold values from 0 to 1
- cost: bfloat16 [64, 512, 1024], P('tiles'), may hold values from -4 to 4
- mask: int32 [64, 64, 8], P('tiles'), may hold values 0 or 1
- tile_adv: int32 [64], P('tiles'), may hold values from -1 to 31, as said below
- tile_slot: int32 [64], P('tiles'), may hold values from -1 to 31
- adv_dual: float32 [32, 512], P('tiles'), may hold values from 0 to 2
- slot_dual: float32 [32, 1024], P('tiles'), may hold values from 0 to 2
- spend_limit: float32 [32, 512], P('tiles'), may hold values from 204 to 921
- capacity: float32 [32, 1024], P('tiles'), may hold values from 64 to 384
Outputs:
- primal: float32 [64, 512, 1024], P('tiles')
- adv_out: float32 [32, 512], P('tiles')
- slot_out: float32 [32, 1024], P('tiles')
The draws below stay inside these ranges and needn't reach their ends.
Inputs may be any that keep to these rules, and one draw needn't show every extreme that they name: -1 marks an empty tile slot; tile_adv and tile_slot are -1 at the same slots. Each device's 2 slots hold 1 to 2 tiles, in its first slots, and some device holds exactly 2.
All inputs are finite; a program needn't handle non-finite values. No bound on the sum of `mask` on one device may be relied on, other than what follows from the above.
Results may differ from the reference program's by a relative error of at most 0.0003.
Values sent between devices are 32-bit elements; how exact they have to be, the bound alone decides.
A program may use at most 64 MiB of HBM per device.

```python
import jax
import jax.numpy as jnp
from jax import lax

ROWS = 512
COLS = 1024
MB_ROWS = 8
MB_COLS = 128
ITERS = 2
CAP = 2
TILE_SLOTS = 64
ADV_BLOCKS = 32
SLOT_BLOCKS = 32
MASK_R = 64
MASK_C = 8


def tile_layout(key):
    base = jax.random.fold_in(key, 11)
    subkeys = jax.random.split(base, 6)
    owners = TILE_SLOTS // CAP
    drawn = jax.random.randint(subkeys[0], (owners,), 0, 5)
    counts = jnp.where(drawn < 3, 1, jnp.where(drawn < 4, min(2, CAP), CAP))
    fuller = jax.random.randint(subkeys[1], (), 0, owners)
    counts = jnp.where(jnp.arange(owners) == fuller, CAP, counts)
    places = jnp.arange(CAP)
    occupied = (places[None, :] < counts[:, None]).reshape(TILE_SLOTS)
    adv_drawn = jax.random.randint(subkeys[2], (TILE_SLOTS,), 0, ADV_BLOCKS)
    hot_blocks = jax.random.randint(subkeys[3], (4,), 0, SLOT_BLOCKS)
    choose = jax.random.randint(subkeys[4], (TILE_SLOTS,), 0, 8)
    spread = jax.random.randint(subkeys[5], (TILE_SLOTS,), 0, SLOT_BLOCKS)
    slot_drawn = jnp.where(choose < 4, hot_blocks[jnp.minimum(choose, 3)], spread)
    adv_ids = jnp.where(occupied, adv_drawn, -1).astype(jnp.int32)
    slot_ids = jnp.where(occupied, slot_drawn, -1).astype(jnp.int32)
    return (adv_ids, slot_ids)


def draw_tile_adv(key, part):
    return tile_layout(key)[0]


def draw_tile_slot(key, part):
    return tile_layout(key)[1]


def place_ends(array, key, low, high):
    index_at = [jax.random.randint(jax.random.fold_in(key, axis), (), 0, length) for axis, length in enumerate(array.shape)]
    main_axis = array.shape.index(max(array.shape))
    beside = index_at[:main_axis] + [(index_at[main_axis] + 1) % array.shape[main_axis]] + index_at[main_axis + 1:]
    return array.at[tuple(index_at)].set(low).at[tuple(beside)].set(high)


def levels(stream_key, shape, pieces, low, high):
    def one(axis_at, parts):
        draws = jax.random.uniform(jax.random.fold_in(jax.random.fold_in(stream_key, 6), axis_at), (parts,), jnp.float32, low / len(pieces), high / len(pieces))
        return jnp.repeat(jnp.exp(draws), shape[axis_at] // parts).reshape((-1,) + (1,) * (len(shape) - axis_at - 1))

    gain = one(*pieces[0])
    for cut in pieces[1:]:
        gain = gain * one(*cut)
    return gain


def bell_draw(rng, extent, scale, bound, cuts=(), kind=jnp.bfloat16):
    entries = scale * jax.random.normal(rng, extent, jnp.float32)
    if cuts:
        entries = entries * levels(rng, extent, cuts, -0.22, 0.18)
    return jnp.clip(entries, -bound, bound).astype(kind)


def setup_inputs(seed: int = 0) -> dict:
    streams_of = jax.random.split(jax.random.key(seed), 10)
    return {
        "primal_start": jnp.clip(1.0 * jax.random.uniform(streams_of[0], (TILE_SLOTS, ROWS, COLS), jnp.float32) ** levels(streams_of[0], (TILE_SLOTS, ROWS, COLS), ((0, 32),), -0.2, 0.2), 0.0, 1.0),
        "cost": bell_draw(streams_of[1], (TILE_SLOTS, ROWS, COLS), 1.0, 4.0, ((0, 32),)),
        "mask": place_ends((jax.random.randint(streams_of[2], (TILE_SLOTS, MASK_R, MASK_C), 0, 4) < 3).astype(jnp.int32), jax.random.fold_in(streams_of[2], 1), 0, 1),
        "tile_adv": draw_tile_adv(jax.random.fold_in(streams_of[9], 71), 0),
        "tile_slot": draw_tile_slot(jax.random.fold_in(streams_of[9], 71), 0),
        "adv_dual": jnp.clip(2.0 * jax.random.uniform(streams_of[5], (ADV_BLOCKS, ROWS), jnp.float32) ** levels(streams_of[5], (ADV_BLOCKS, ROWS), ((0, 32),), -0.2, 0.2), 0.0, 2.0),
        "slot_dual": jnp.clip(2.0 * jax.random.uniform(streams_of[6], (SLOT_BLOCKS, COLS), jnp.float32) ** levels(streams_of[6], (SLOT_BLOCKS, COLS), ((0, 32),), -0.2, 0.2), 0.0, 2.0),
        "spend_limit": jnp.clip(204.0 + 717.0 * jax.random.uniform(streams_of[7], (ADV_BLOCKS, ROWS), jnp.float32) ** levels(streams_of[7], (ADV_BLOCKS, ROWS), ((0, 32),), -0.2, 0.2), 204.0, 921.0),
        "capacity": jnp.clip(64.0 + 320.0 * jax.random.uniform(streams_of[8], (SLOT_BLOCKS, COLS), jnp.float32) ** levels(streams_of[8], (SLOT_BLOCKS, COLS), ((0, 32),), -0.2, 0.2), 64.0, 384.0),
    }


tau_step = 0.5


def expand_mask(blocks):
    values = blocks.astype(jnp.float32)
    rows_in = values.shape[-2]
    cols_in = values.shape[-1]
    shaped = jnp.broadcast_to(values[..., :, None, :, None], values.shape[:-2] + (rows_in, MB_ROWS, cols_in, MB_COLS))
    return shaped.reshape(values.shape[:-2] + (rows_in * MB_ROWS, cols_in * MB_COLS))


def reference(primal_start, cost, mask, tile_adv, tile_slot, adv_dual, slot_dual, spend_limit, capacity):
    highest = lax.Precision.HIGHEST
    adv_onehot = (tile_adv[:, None] == jnp.arange(ADV_BLOCKS, dtype=jnp.int32)[None, :]).astype(jnp.float32)
    slot_onehot = (tile_slot[:, None] == jnp.arange(SLOT_BLOCKS, dtype=jnp.int32)[None, :]).astype(jnp.float32)
    present = (tile_adv >= 0).astype(jnp.float32)
    primal = primal_start
    for sweep_index in range(ITERS):
        adv_rows = jnp.dot(adv_onehot, adv_dual, precision=highest)
        slot_cols = jnp.dot(slot_onehot, slot_dual, precision=highest)
        first_sweep = sweep_index == 0

        def tile_step(items):
            previous, price, blocks, alive_flag, adv_row, slot_col = items
            weight = expand_mask(blocks) * alive_flag
            if first_sweep:
                previous = weight * previous
            update = weight * jnp.clip(previous - tau_step * (price.astype(jnp.float32) + adv_row[:, None] + slot_col[None, :]), 0.0, 1.0)
            extended = 2.0 * update - previous
            return update, jnp.sum(extended, axis=1), jnp.sum(extended, axis=0)

        primal, row_sums, col_sums = lax.map(tile_step, (primal, cost, mask, present, adv_rows, slot_cols))
        row_use = jnp.dot(adv_onehot.T, row_sums, precision=highest)
        col_use = jnp.dot(slot_onehot.T, col_sums, precision=highest)
        adv_dual = jnp.maximum(adv_dual + (row_use - spend_limit) / COLS, 0.0)
        slot_dual = jnp.maximum(slot_dual + (col_use - capacity) / ROWS, 0.0)
    return primal, adv_dual, slot_dual
```

```python
import functools

import jax
import jax.numpy as jnp
from jax import lax
from jax.experimental import pallas as pl
from jax.experimental.pallas import tpu as pltpu
from jax.sharding import PartitionSpec as P

ITERS = 2
LANES = 128
SUB = 8
STEP = 32
MESH = pl.DeviceIdType.MESH


def split_chips(chips):
    inner = 1
    for size in range(1, chips + 1):
        if size * size <= chips and chips % size == 0:
            inner = size
    return chips // inner, inner


class Gather:
    def __init__(self, buf, outer_sems, inner_sems, core_sems, place, sizes):
        self.buf = buf
        self.outer_sems, self.inner_sems, self.core_sems = outer_sems, inner_sems, core_sems
        self.o, self.i, self.c = place
        self.outer, self.inner = sizes
        self.sent = []

    def device(self, o, i, c):
        return ((o * self.inner + i) * 2 + c,)

    def back(self, at, k, size):
        return lax.rem(at - k + size, size)

    def copy(self, ref, sems, k, device, start):
        made = pltpu.make_async_remote_copy(
            src_ref=ref,
            dst_ref=ref,
            send_sem=sems.at[0, k],
            recv_sem=sems.at[1, k],
            device_id=device,
            device_id_type=MESH,
        )
        if start:
            made.start()
            self.sent.append(made)
        return made

    def start(self):
        for k in range(1, self.outer):
            to = self.device(lax.rem(self.o + k, self.outer), self.i, self.c)
            self.copy(self.buf.at[self.c, self.i, self.o], self.outer_sems, k, to, True)

    def to_partner(self, k):
        column = self.buf.at[self.c, self.back(self.i, k, self.inner)]
        self.copy(column, self.core_sems, k, self.device(self.o, self.i, 1 - self.c), True)

    def spread(self):
        for k in range(1, self.outer):
            block = self.buf.at[self.c, self.i, self.back(self.o, k, self.outer)]
            self.copy(block, self.outer_sems, k, self.device(self.o, self.i, 1 - self.c), False).wait_recv()
        for k in range(1, self.inner):
            to = self.device(self.o, lax.rem(self.i + k, self.inner), self.c)
            self.copy(self.buf.at[self.c, self.i], self.inner_sems, k, to, True)
        self.to_partner(0)

    def pass_on(self):
        for k in range(1, self.inner):
            column = self.buf.at[self.c, self.back(self.i, k, self.inner)]
            self.copy(column, self.inner_sems, k, self.device(self.o, self.i, 1 - self.c), False).wait_recv()
            self.to_partner(k)

    def finish(self):
        for k in range(self.inner):
            column = self.buf.at[1 - self.c, self.back(self.i, k, self.inner)]
            self.copy(column, self.core_sems, k, self.device(self.o, self.i, 1 - self.c), False).wait_recv()

    def drain(self):
        for made in self.sent:
            made.wait_send()


def kernel(
    outer, inner, cap, rows, cols,
    adv_id, slot_id, mask, adv_dual, slot_dual, limit, capacity, start_hbm, cost_hbm,
    primal_hbm, adv_out, slot_out,
    tile, price, weight, row_part, col_sum, row_sum, half_adv, half_slot, totals,
    dual_buf, rest_buf, sums_one, sums_two,
    outer_sems, inner_sems, core_sems, in_sems, out_sems,
):
    me = lax.axis_index("tiles")
    c = lax.rem(me, 2)
    i = lax.rem(me // 2, inner)
    o = me // (2 * inner)
    row_lines, col_lines = rows // LANES, cols // LANES
    groups = STEP // SUB
    mask_rows = mask.shape[1]

    loads = []
    for t in range(cap):
        pair = (
            pltpu.make_async_copy(start_hbm.at[t], tile.at[t], in_sems.at[0, t]),
            pltpu.make_async_copy(cost_hbm.at[t], price.at[t], in_sems.at[1, t]),
        )
        for made in pair:
            made.start()
        loads.append(pair)

    barrier = pltpu.get_barrier_semaphore()
    peers = [((lax.rem(o + k, outer) * inner + i) * 2 + c) for k in range(1, outer)]
    peers += [((o * inner + lax.rem(i + k, inner)) * 2 + c) for k in range(1, inner)]
    peers += [(o * inner + i) * 2 + 1 - c]
    for peer in peers:
        pl.semaphore_signal(barrier, inc=1, device_id=(peer,), device_id_type=MESH)

    gathers = [
        Gather(buf, outer_sems.at[g], inner_sems.at[g], core_sems.at[g], (o, i, c), (outer, inner))
        for g, buf in enumerate((dual_buf, rest_buf, sums_one, sums_two))
    ]
    duals, rest, first, second = gathers

    for r in range(row_lines):
        at = slice(r * LANES, (r + 1) * LANES)
        dual_buf[c, i, o, r:r + 1, :] = adv_dual[0:1, at]
        dual_buf[c, i, o, row_lines + r:row_lines + r + 1, :] = limit[0:1, at]
    for r in range(col_lines):
        at = slice(r * LANES, (r + 1) * LANES)
        dual_buf[c, i, o, 2 * row_lines + r:2 * row_lines + r + 1, :] = slot_dual[0:1, at]
        rest_buf[c, i, o, r:r + 1, :] = capacity[0:1, at]
    for t in range(cap):
        rest_buf[c, i, o, col_lines + t:col_lines + t + 1, :] = jnp.full(
            (1, LANES), adv_id[t].astype(jnp.float32))
        rest_buf[c, i, o, col_lines + cap + t:col_lines + cap + t + 1, :] = jnp.full(
            (1, LANES), slot_id[t].astype(jnp.float32))

    pl.semaphore_wait(barrier, len(peers))
    duals.start()
    rest.start()

    for t in range(cap):
        alive = jnp.where(adv_id[t] >= 0, 1.0, 0.0).astype(jnp.float32)
        blocks = mask[t].astype(jnp.float32) * alive
        for j in range(mask.shape[2]):
            weight[t, j] = jnp.broadcast_to(blocks[:, j:j + 1], (mask_rows, LANES))

    def exists(t, at, j):
        return jnp.broadcast_to(weight[t, j, pl.ds(at, 1), :], (SUB, LANES))

    def sum_tile(t, value):
        def step(s, col):
            col = list(col)
            for g in range(groups):
                row = None
                for j in range(col_lines):
                    piece = value(s, g, j)
                    row = piece if row is None else row + piece
                    col[j] = col[j] + piece
                row_part[t, pl.ds(s * STEP + g * SUB, SUB), :] = row
            return tuple(col)

        zero = jnp.zeros((SUB, LANES), jnp.float32)
        return lax.fori_loop(0, rows // STEP, step, (zero,) * col_lines)

    def keep_sums(slot, t, col):
        for r in range(row_lines):
            turned = jnp.transpose(row_part[t, r * LANES:(r + 1) * LANES, :])
            row_sum[slot, t * row_lines + r:t * row_lines + r + 1, :] = jnp.sum(turned, axis=0, keepdims=True)
        for j in range(col_lines):
            col_sum[slot, t, j:j + 1, :] = jnp.sum(col[j], axis=0, keepdims=True)

    def prepare(t):
        for made in loads[t]:
            made.wait()

        def step(s, col):
            col = list(col)
            for h in range(STEP // 16):
                row = [None, None]
                for j in range(col_lines):
                    at = (t, pl.ds(s * STEP + h * 16, 16), slice(j * LANES, (j + 1) * LANES))
                    x = tile[at]
                    tile[at] = x - 0.5 * price[at].astype(jnp.float32)
                    for half in range(2):
                        piece = x[half * SUB:(half + 1) * SUB] * exists(t, s * groups + h * 2 + half, j)
                        row[half] = piece if row[half] is None else row[half] + piece
                        col[j] = col[j] + piece
                for half in range(2):
                    row_part[t, pl.ds(s * STEP + h * 16 + half * SUB, SUB), :] = row[half]
            return tuple(col)

        zero = jnp.zeros((SUB, LANES), jnp.float32)
        keep_sums(0, t, lax.fori_loop(0, rows // STEP, step, (zero,) * col_lines))

    def less_price(t):
        def step(s, carry):
            for h in range(STEP // 16):
                for j in range(col_lines):
                    at = (t, pl.ds(s * STEP + h * 16, 16), slice(j * LANES, (j + 1) * LANES))
                    tile[at] = tile[at] - 0.5 * price[at].astype(jnp.float32)
            return carry

        lax.fori_loop(0, rows // STEP, step, 0)

    def set_duals(t, adv, slot):
        for r in range(row_lines):
            spread = jnp.broadcast_to(0.5 * adv[r:r + 1, :], (LANES, LANES))
            half_adv[t, r * LANES:(r + 1) * LANES, :] = jnp.transpose(spread)
        half_slot[t] = 0.5 * slot

    def update(t, slot):
        slots = [jnp.broadcast_to(half_slot[t, j:j + 1, :], (SUB, LANES)) for j in range(col_lines)]

        def value(s, g, j):
            at = (t, pl.ds(s * STEP + g * SUB, SUB), slice(j * LANES, (j + 1) * LANES))
            moved = tile[at] - half_adv[t, pl.ds(s * STEP + g * SUB, SUB), :] - slots[j]
            new = jnp.clip(moved, 0.0, 1.0) * exists(t, s * groups + g, j)
            tile[at] = new
            return new

        keep_sums(slot, t, sum_tile(t, value))

    def post(buf, slot):
        buf[c, i, o, 0:cap * row_lines, :] = 2.0 * row_sum[slot] - row_sum[slot - 1]
        for t in range(cap):
            at = cap * row_lines + t * col_lines
            buf[c, i, o, at:at + col_lines, :] = 2.0 * col_sum[slot, t] - col_sum[slot - 1, t]

    def add_up(buf, targets):
        wanted = [
            (jnp.full((1, LANES), a.astype(jnp.float32)), jnp.full((1, LANES), b.astype(jnp.float32)))
            for a, b in targets
        ]

        def step(m, sums):
            sums = list(sums)
            cc, ii = m // inner, lax.rem(m, inner)
            for oo in range(outer):
                for t in range(cap):
                    a_of = rest_buf[cc, ii, oo, col_lines + t:col_lines + t + 1, :]
                    s_of = rest_buf[cc, ii, oo, col_lines + cap + t:col_lines + cap + t + 1, :]
                    by_row = buf[cc, ii, oo, t * row_lines:(t + 1) * row_lines, :]
                    at = cap * row_lines + t * col_lines
                    by_col = buf[cc, ii, oo, at:at + col_lines, :]
                    for k, (a, b) in enumerate(wanted):
                        hit_a = jnp.where(a_of == a, 1.0, 0.0)
                        hit_b = jnp.where(s_of == b, 1.0, 0.0)
                        sums[2 * k] = sums[2 * k] + by_row * hit_a
                        sums[2 * k + 1] = sums[2 * k + 1] + by_col * hit_b
            return tuple(sums)

        begin = []
        for _ in targets:
            begin += [jnp.zeros((row_lines, LANES), jnp.float32), jnp.zeros((col_lines, LANES), jnp.float32)]
        return lax.fori_loop(0, 2 * inner, step, tuple(begin))

    def place(block):
        return lax.rem(block, 2), lax.rem(block // 2, inner), block // (2 * inner)

    def old_adv(block):
        at = place(block)
        return dual_buf[at + (slice(0, row_lines),)], dual_buf[at + (slice(row_lines, 2 * row_lines),)]

    def old_slot(block):
        at = place(block)
        return dual_buf[at + (slice(2 * row_lines, 2 * row_lines + col_lines),)], rest_buf[at + (slice(0, col_lines),)]

    ids = [(jnp.maximum(adv_id[t], 0), jnp.maximum(slot_id[t], 0)) for t in range(cap)]

    prepare(0)
    duals.spread()
    rest.spread()
    for t in range(1, cap):
        prepare(t)
    duals.pass_on()
    duals.finish()

    for t in range(cap):
        set_duals(t, old_adv(ids[t][0])[0], old_slot(ids[t][1])[0])
    for t in range(cap):
        update(t, 1)
    post(sums_one, 1)
    first.start()
    rest.pass_on()
    less_price(0)
    first.spread()
    for t in range(1, cap):
        less_price(t)
    first.pass_on()
    rest.finish()
    first.finish()

    targets = ids + [(me, me)]
    sums = add_up(sums_one, targets)
    for k, (a, b) in enumerate(targets):
        adv, lim = old_adv(a)
        slot, room = old_slot(b)
        adv = jnp.maximum(adv + (sums[2 * k] - lim) / cols, 0.0)
        slot = jnp.maximum(slot + (sums[2 * k + 1] - room) / rows, 0.0)
        if k < cap:
            set_duals(k, adv, slot)
        else:
            totals[0:row_lines, :] = adv
            totals[row_lines:row_lines + col_lines, :] = slot

    stores = []
    for t in range(cap):
        update(t, 2)
        made = pltpu.make_async_copy(tile.at[t], primal_hbm.at[t], out_sems.at[t])
        made.start()
        stores.append(made)
    post(sums_two, 2)
    second.start()
    second.spread()
    second.pass_on()
    second.finish()

    row_use, col_use = add_up(sums_two, [(me, me)])
    adv = jnp.maximum(totals[0:row_lines, :] + (row_use - old_adv(me)[1]) / cols, 0.0)
    slot = jnp.maximum(
        totals[row_lines:row_lines + col_lines, :] + (col_use - old_slot(me)[1]) / rows, 0.0)
    for r in range(row_lines):
        adv_out[0:1, r * LANES:(r + 1) * LANES] = adv[r:r + 1, :]
    for r in range(col_lines):
        slot_out[0:1, r * LANES:(r + 1) * LANES] = slot[r:r + 1, :]

    for gather in gathers:
        gather.drain()
    for made in stores:
        made.wait()


def body(primal_start, cost, mask, tile_adv, tile_slot, adv_dual, slot_dual, spend_limit, capacity):
    devices = lax.axis_size("tiles")
    outer, inner = split_chips(devices // 2)
    cap, rows, cols = primal_start.shape
    row_lines, col_lines = rows // LANES, cols // LANES
    f32 = jnp.float32
    spread = (2, inner, outer)
    dual_lines = 2 * row_lines + col_lines
    rest_lines = col_lines + -(-2 * cap // SUB) * SUB
    sum_lines = cap * (row_lines + col_lines)
    vmem = pl.BlockSpec(memory_space=pltpu.VMEM)
    smem = pl.BlockSpec(memory_space=pltpu.SMEM)
    hbm = pl.BlockSpec(memory_space=pl.ANY)
    return pl.pallas_call(
        functools.partial(kernel, outer, inner, cap, rows, cols),
        out_shape=(
            jax.ShapeDtypeStruct(primal_start.shape, f32),
            jax.ShapeDtypeStruct(adv_dual.shape, f32),
            jax.ShapeDtypeStruct(slot_dual.shape, f32),
        ),
        in_specs=[smem, smem, vmem, vmem, vmem, vmem, vmem, hbm, hbm],
        out_specs=(hbm, vmem, vmem),
        scratch_shapes=[
            pltpu.VMEM((cap, rows, cols), f32),
            pltpu.VMEM((cap, rows, cols), cost.dtype),
            pltpu.VMEM((cap, mask.shape[2], mask.shape[1], LANES), f32),
            pltpu.VMEM((cap, rows, LANES), f32),
            pltpu.VMEM((ITERS + 1, cap, col_lines, LANES), f32),
            pltpu.VMEM((ITERS + 1, cap * row_lines, LANES), f32),
            pltpu.VMEM((cap, rows, LANES), f32),
            pltpu.VMEM((cap, col_lines, LANES), f32),
            pltpu.VMEM((row_lines + col_lines, LANES), f32),
            pltpu.VMEM(spread + (dual_lines, LANES), f32),
            pltpu.VMEM(spread + (rest_lines, LANES), f32),
            pltpu.VMEM(spread + (sum_lines, LANES), f32),
            pltpu.VMEM(spread + (sum_lines, LANES), f32),
            pltpu.SemaphoreType.DMA((4, 2, outer)),
            pltpu.SemaphoreType.DMA((4, 2, inner)),
            pltpu.SemaphoreType.DMA((4, 2, inner)),
            pltpu.SemaphoreType.DMA((2, cap)),
            pltpu.SemaphoreType.DMA((cap,)),
        ],
        compiler_params=pltpu.CompilerParams(
            collective_id=0, has_side_effects=True, vmem_limit_bytes=40 * 1024 * 1024
        ),
    )(tile_adv, tile_slot, mask, adv_dual, slot_dual, spend_limit, capacity, primal_start, cost)


def solution(mesh):
    return jax.shard_map(
        body,
        mesh=mesh,
        in_specs=(
            P("tiles", None, None),
            P("tiles", None, None),
            P("tiles", None, None),
            P("tiles"),
            P("tiles"),
            P("tiles", None),
            P("tiles", None),
            P("tiles", None),
            P("tiles", None),
        ),
        out_specs=(P("tiles", None, None), P("tiles", None), P("tiles", None)),
        check_vma=False,
    )
```

```python
import functools

import jax
import jax.numpy as jnp
from jax import lax
from jax.experimental import pallas as pl
from jax.experimental.pallas import tpu as pltpu
from jax.sharding import PartitionSpec as P

ITERS = 2
LANES = 128
SUB = 8
STEP = 32
MESH = pl.DeviceIdType.MESH


def split_chips(chips):
    inner = 1
    for size in range(1, chips + 1):
        if size * size <= chips and chips % size == 0:
            inner = size
    return chips // inner, inner


class Copies:
    def __init__(self, sems):
        self.sems = sems
        self.made = {}

    def start(self, k, src, dst, device):
        made = pltpu.make_async_remote_copy(
            src_ref=src,
            dst_ref=dst,
            send_sem=self.sems.at[0, k],
            recv_sem=self.sems.at[1, k],
            device_id=(device,),
            device_id_type=MESH,
        )
        made.start()
        self.made[k] = made

    def arrive(self):
        for made in self.made.values():
            made.wait_recv()

    def drain(self):
        for made in self.made.values():
            made.wait_send()


def kernel(
    outer, inner, cap, rows, cols,
    adv_id, slot_id, mask_hbm, adv_hbm, slot_hbm, limit_hbm, room_hbm, start_hbm, cost_hbm,
    primal_hbm, adv_out, slot_out,
    tile, price, blocks, adv_dual, slot_dual, limit, capacity, square, weight, row_part, col_sum, row_sum,
    half_adv, half_slot, totals, dual_buf, rest_buf, sums_one, sums_two, ids_buf,
    send_start, send_one, send_two, got_start, got_one, got_two,
    column_sems, plane_sems, in_sems, small_sems, out_sems,
):
    plane = 2 * inner
    me = lax.axis_index("tiles")
    p = lax.rem(me, plane)
    o = me // plane
    row_lines, col_lines = rows // LANES, cols // LANES
    groups = STEP // SUB
    mask_rows, mask_cols = mask_hbm.shape[2], mask_hbm.shape[1]

    small = [
        pltpu.make_async_copy(src, dst, small_sems.at[n])
        for n, (src, dst) in enumerate((
            (adv_hbm, adv_dual), (slot_hbm, slot_dual), (limit_hbm, limit), (room_hbm, capacity), (mask_hbm, blocks)))
    ]
    for made in small:
        made.start()
    loads = []
    for t in range(cap):
        pair = (
            pltpu.make_async_copy(start_hbm.at[t], tile.at[t], in_sems.at[0, t]),
            pltpu.make_async_copy(cost_hbm.at[t], price.at[t], in_sems.at[1, t]),
        )
        for made in pair:
            made.start()
        loads.append(pair)

    def in_column(k):
        return lax.rem(o + k, outer) * plane + p

    def in_plane(k):
        return o * plane + lax.rem(p + k, plane)

    barrier = pltpu.get_barrier_semaphore()
    peers = [in_column(k) for k in range(1, outer)] + [in_plane(k) for k in range(1, plane)]
    for peer in peers:
        pl.semaphore_signal(barrier, inc=1, device_id=(peer,), device_id_type=MESH)

    exchanges = [Copies(column_sems.at[g]) for g in range(4)] + [Copies(plane_sems.at[g]) for g in range(4)]
    duals, rest, first, second, named, part_start, part_one, part_two = exchanges

    def slot_at(e):
        return slice(e * col_lines, (e + 1) * col_lines)

    def adv_at(n, e):
        return slice(n * col_lines + e * row_lines, n * col_lines + (e + 1) * row_lines)

    id_line = col_lines + row_lines
    for t in range(cap):
        for n, ids in ((t, adv_id), (cap + t, slot_id)):
            value = jnp.full((1, LANES), ids[t].astype(jnp.float32))
            ids_buf[p, n:n + 1, :] = value
            rest_buf[o, id_line + n:id_line + n + 1, :] = value
    for made in small[:4]:
        made.wait()
    for r in range(row_lines):
        at = slice(r * LANES, (r + 1) * LANES)
        dual_buf[o, col_lines + r:col_lines + r + 1, :] = adv_dual[0:1, at]
        rest_buf[o, col_lines + r:col_lines + r + 1, :] = limit[0:1, at]
    for r in range(col_lines):
        at = slice(r * LANES, (r + 1) * LANES)
        dual_buf[o, r:r + 1, :] = slot_dual[0:1, at]
        rest_buf[o, r:r + 1, :] = capacity[0:1, at]

    def send_column(copies, buf):
        for k in range(outer - 1, 0, -1):
            copies.start(k, buf.at[o], buf.at[o], in_column(k))

    pl.semaphore_wait(barrier, len(peers))
    send_column(duals, dual_buf)
    for k in range(1, plane):
        named.start(k, ids_buf.at[p], ids_buf.at[p], in_plane(k))
    send_column(rest, rest_buf)

    small[4].wait()
    square[...] = jnp.zeros_like(square)
    for t in range(cap):
        alive = jnp.where(adv_id[t] >= 0, 1.0, 0.0).astype(jnp.float32)
        square[0:mask_cols, 0:mask_rows] = blocks[t].astype(jnp.float32) * alive
        turned = jnp.transpose(square[...])
        for j in range(mask_cols):
            weight[t, j] = jnp.broadcast_to(turned[0:mask_rows, j:j + 1], (mask_rows, LANES))

    def exists(t, at, j):
        return jnp.broadcast_to(weight[t, j, pl.ds(at, 1), :], (SUB, LANES))

    def sum_tile(t, value):
        def step(s, col):
            col = list(col)
            for g in range(groups):
                row = None
                for j in range(col_lines):
                    piece = value(s, g, j)
                    row = piece if row is None else row + piece
                    col[j] = col[j] + piece
                row_part[t, pl.ds(s * STEP + g * SUB, SUB), :] = row
            return tuple(col)

        zero = jnp.zeros((SUB, LANES), jnp.float32)
        return lax.fori_loop(0, rows // STEP, step, (zero,) * col_lines)

    def keep_sums(slot, t, col):
        for r in range(row_lines):
            turned = jnp.transpose(row_part[t, r * LANES:(r + 1) * LANES, :])
            row_sum[slot, t * row_lines + r:t * row_lines + r + 1, :] = jnp.sum(turned, axis=0, keepdims=True)
        for j in range(col_lines):
            col_sum[slot, t, j:j + 1, :] = jnp.sum(col[j], axis=0, keepdims=True)

    def prepare(t):
        for made in loads[t]:
            made.wait()

        def step(s, col):
            col = list(col)
            for h in range(STEP // 16):
                row = [None, None]
                for j in range(col_lines):
                    at = (t, pl.ds(s * STEP + h * 16, 16), slice(j * LANES, (j + 1) * LANES))
                    x = tile[at]
                    tile[at] = x - 0.5 * price[at].astype(jnp.float32)
                    for half in range(2):
                        piece = x[half * SUB:(half + 1) * SUB] * exists(t, s * groups + h * 2 + half, j)
                        row[half] = piece if row[half] is None else row[half] + piece
                        col[j] = col[j] + piece
                for half in range(2):
                    row_part[t, pl.ds(s * STEP + h * 16 + half * SUB, SUB), :] = row[half]
            return tuple(col)

        zero = jnp.zeros((SUB, LANES), jnp.float32)
        keep_sums(0, t, lax.fori_loop(0, rows // STEP, step, (zero,) * col_lines))

    def less_price(t):
        def step(s, carry):
            for h in range(STEP // 16):
                for j in range(col_lines):
                    at = (t, pl.ds(s * STEP + h * 16, 16), slice(j * LANES, (j + 1) * LANES))
                    tile[at] = tile[at] - 0.5 * price[at].astype(jnp.float32)
            return carry

        lax.fori_loop(0, rows // STEP, step, 0)

    def set_duals(t, adv, slot):
        for r in range(row_lines):
            spread = jnp.broadcast_to(0.5 * adv[r:r + 1, :], (LANES, LANES))
            half_adv[t, r * LANES:(r + 1) * LANES, :] = jnp.transpose(spread)
        half_slot[t] = 0.5 * slot

    def update(t, slot):
        slots = [jnp.broadcast_to(half_slot[t, j:j + 1, :], (SUB, LANES)) for j in range(col_lines)]

        def value(s, g, j):
            at = (t, pl.ds(s * STEP + g * SUB, SUB), slice(j * LANES, (j + 1) * LANES))
            moved = tile[at] - half_adv[t, pl.ds(s * STEP + g * SUB, SUB), :] - slots[j]
            new = jnp.clip(moved, 0.0, 1.0) * exists(t, s * groups + g, j)
            tile[at] = new
            return new

        keep_sums(slot, t, sum_tile(t, value))

    def post(buf, slot):
        for t in range(cap):
            at = slice(t * row_lines, (t + 1) * row_lines)
            buf[o, slot_at(t), :] = 2.0 * col_sum[slot, t] - col_sum[slot - 1, t]
            buf[o, adv_at(cap, t), :] = 2.0 * row_sum[slot, at, :] - row_sum[slot - 1, at, :]

    def splat(value):
        return jnp.full((1, LANES), value.astype(jnp.float32))

    def tile_items(buf):
        return [
            (
                rest_buf[b, id_line + t:id_line + t + 1, :], rest_buf[b, id_line + cap + t:id_line + cap + t + 1, :],
                buf[b, adv_at(cap, t), :], buf[b, slot_at(t), :],
            )
            for b in range(outer) for t in range(cap)
        ]

    def block_items(buf, sign):
        return [
            (splat(b * plane + p), splat(b * plane + p), sign * buf[b, adv_at(1, 0), :], sign * buf[b, slot_at(0), :])
            for b in range(outer)
        ]

    def targets_of(q, own):
        found = []
        if own != "alone":
            found = [(ids_buf[q, t:t + 1, :], ids_buf[q, cap + t:cap + t + 1, :]) for t in range(cap)]
        if own:
            found.append((splat(o * plane + q),) * 2)
        return found

    def part(items, targets, into, add):
        n = len(targets)
        for e, (a, b) in enumerate(targets):
            adv = into[adv_at(n, e), :] if add else jnp.zeros((row_lines, LANES), jnp.float32)
            slot = into[slot_at(e), :] if add else jnp.zeros((col_lines, LANES), jnp.float32)
            for a_of, b_of, by_row, by_col in items:
                adv = adv + jnp.where(a_of == a, 1.0, 0.0) * by_row
                slot = slot + jnp.where(b_of == b, 1.0, 0.0) * by_col
            into[adv_at(n, e), :] = adv
            into[slot_at(e), :] = slot

    def parts(copies, items, own, send, got, add=False, go=True):
        order = list(range(plane - 1, -1, -1))
        for k in order:
            into = send.at[k] if k else got.at[0]
            part(items, targets_of(lax.rem(p + k, plane), own), into, add)
            if go and k:
                copies.start(k, send.at[k], got.at[k], in_plane(k))

    def total(got):
        value = got[0]
        for k in range(1, plane):
            value = value + got[k]
        return value

    prepare(0)
    named.arrive()
    duals.arrive()
    parts(part_start, block_items(dual_buf, 1.0), False, send_start, got_start)
    for t in range(1, cap):
        prepare(t)
    rest.arrive()
    part_start.arrive()

    old = total(got_start)
    for t in range(cap):
        set_duals(t, old[adv_at(cap, t)], old[slot_at(t)])
    for t in range(cap):
        update(t, 1)
    post(sums_one, 1)
    send_column(first, sums_one)
    parts(part_one, block_items(rest_buf, -1.0), True, send_one, got_one, go=False)
    less_price(0)
    first.arrive()
    parts(part_one, tile_items(sums_one), True, send_one, got_one, add=True)
    for t in range(1, cap):
        less_price(t)
    part_one.arrive()

    moved = total(got_one)
    for k in range(cap + 1):
        adv, slot = moved[adv_at(cap + 1, k)], moved[slot_at(k)]
        if k < cap:
            adv = jnp.maximum(old[adv_at(cap, k)] + adv / cols, 0.0)
            slot = jnp.maximum(old[slot_at(k)] + slot / rows, 0.0)
            set_duals(k, adv, slot)
        else:
            totals[adv_at(1, 0), :] = jnp.maximum(dual_buf[o, adv_at(1, 0), :] + adv / cols, 0.0)
            totals[slot_at(0), :] = jnp.maximum(dual_buf[o, slot_at(0), :] + slot / rows, 0.0)

    stores = []
    for t in range(cap):
        update(t, 2)
        made = pltpu.make_async_copy(tile.at[t], primal_hbm.at[t], out_sems.at[t])
        made.start()
        stores.append(made)
    post(sums_two, 2)
    send_column(second, sums_two)
    second.arrive()
    parts(part_two, tile_items(sums_two), "alone", send_two, got_two)
    part_two.arrive()

    use = total(got_two)
    adv = totals[adv_at(1, 0), :] + (use[adv_at(1, 0)] - rest_buf[o, adv_at(1, 0), :]) / cols
    slot = totals[slot_at(0), :] + (use[slot_at(0)] - rest_buf[o, slot_at(0), :]) / rows
    for r in range(row_lines):
        adv_out[0:1, r * LANES:(r + 1) * LANES] = jnp.maximum(adv[r:r + 1, :], 0.0)
    for r in range(col_lines):
        slot_out[0:1, r * LANES:(r + 1) * LANES] = jnp.maximum(slot[r:r + 1, :], 0.0)

    for copies in exchanges:
        copies.drain()
    for made in stores:
        made.wait()


def store(*refs):
    pieces = refs[-1].shape[0] - 2
    cap, rows = refs[0].shape[:2]
    size = cap * rows // pieces
    made = []
    for n in range(pieces):
        at = (n * size // rows, pl.ds(n * size % rows, size))
        made.append(pltpu.make_async_copy(refs[0].at[at], refs[3].at[at], refs[-1].at[n]))
    made.append(pltpu.make_async_copy(refs[1], refs[4], refs[-1].at[pieces]))
    made.append(pltpu.make_async_copy(refs[2], refs[5], refs[-1].at[pieces + 1]))
    for copy in made:
        copy.start()
    for copy in made:
        copy.wait()


def body(primal_start, cost, mask, tile_adv, tile_slot, adv_dual, slot_dual, spend_limit, capacity):
    devices = lax.axis_size("tiles")
    outer, inner = split_chips(devices // 2)
    plane = 2 * inner
    cap, rows, cols = primal_start.shape
    row_lines, col_lines = rows // LANES, cols // LANES
    entry = row_lines + col_lines
    f32 = jnp.float32
    vmem = pl.BlockSpec(memory_space=pltpu.VMEM)
    smem = pl.BlockSpec(memory_space=pltpu.SMEM)
    hbm = pl.BlockSpec(memory_space=pltpu.HBM)
    mask = jnp.swapaxes(mask, 1, 2)
    outs = (
        jax.ShapeDtypeStruct(primal_start.shape, f32),
        jax.ShapeDtypeStruct(adv_dual.shape, f32),
        jax.ShapeDtypeStruct(slot_dual.shape, f32),
    )
    results = pl.pallas_call(
        functools.partial(kernel, outer, inner, cap, rows, cols),
        out_shape=outs,
        in_specs=[smem, smem, hbm, hbm, hbm, hbm, hbm, hbm, hbm],
        out_specs=(hbm, vmem, vmem),
        scratch_shapes=[
            pltpu.VMEM((cap, rows, cols), f32),
            pltpu.VMEM((cap, rows, cols), cost.dtype),
            pltpu.VMEM(mask.shape, mask.dtype),
            pltpu.VMEM(adv_dual.shape, f32),
            pltpu.VMEM(slot_dual.shape, f32),
            pltpu.VMEM(spend_limit.shape, f32),
            pltpu.VMEM(capacity.shape, f32),
            pltpu.VMEM((LANES, LANES), f32),
            pltpu.VMEM((cap, mask.shape[1], mask.shape[2], LANES), f32),
            pltpu.VMEM((cap, rows, LANES), f32),
            pltpu.VMEM((ITERS + 1, cap, col_lines, LANES), f32),
            pltpu.VMEM((ITERS + 1, cap * row_lines, LANES), f32),
            pltpu.VMEM((cap, rows, LANES), f32),
            pltpu.VMEM((cap, col_lines, LANES), f32),
            pltpu.VMEM((entry, LANES), f32),
            pltpu.VMEM((outer, entry, LANES), f32),
            pltpu.VMEM((outer, entry + 2 * cap, LANES), f32),
            pltpu.VMEM((outer, cap * entry, LANES), f32),
            pltpu.VMEM((outer, cap * entry, LANES), f32),
            pltpu.VMEM((plane, 2 * cap, LANES), f32),
            pltpu.VMEM((plane, cap * entry, LANES), f32),
            pltpu.VMEM((plane, (cap + 1) * entry, LANES), f32),
            pltpu.VMEM((plane, entry, LANES), f32),
            pltpu.VMEM((plane, cap * entry, LANES), f32),
            pltpu.VMEM((plane, (cap + 1) * entry, LANES), f32),
            pltpu.VMEM((plane, entry, LANES), f32),
            pltpu.SemaphoreType.DMA((4, 2, outer)),
            pltpu.SemaphoreType.DMA((4, 2, plane)),
            pltpu.SemaphoreType.DMA((2, cap)),
            pltpu.SemaphoreType.DMA((5,)),
            pltpu.SemaphoreType.DMA((cap,)),
        ],
        compiler_params=pltpu.CompilerParams(
            collective_id=0, has_side_effects=True, vmem_limit_bytes=60 * 1024 * 1024
        ),
    )(tile_adv, tile_slot, mask, adv_dual, slot_dual, spend_limit, capacity, primal_start, cost)
    return pl.pallas_call(
        store,
        out_shape=outs,
        in_specs=[pl.BlockSpec(memory_space=pl.ANY)] * len(outs),
        out_specs=(hbm,) * len(outs),
        scratch_shapes=[pltpu.SemaphoreType.DMA((4 * cap + 2,))],
        compiler_params=pltpu.CompilerParams(vmem_limit_bytes=60 * 1024 * 1024),
    )(*results)


def solution(mesh):
    return jax.shard_map(
        body,
        mesh=mesh,
        in_specs=(
            P("tiles", None, None),
            P("tiles", None, None),
            P("tiles", None, None),
            P("tiles"),
            P("tiles"),
            P("tiles", None),
            P("tiles", None),
            P("tiles", None),
            P("tiles", None),
        ),
        out_specs=(P("tiles", None, None), P("tiles", None), P("tiles", None)),
        check_vma=False,
    )
```

```python
import functools

import jax
import jax.numpy as jnp
from jax import lax
from jax.experimental import pallas as pl
from jax.experimental.pallas import tpu as pltpu
from jax.sharding import PartitionSpec as P

ITERS = 2
LANES = 128
SUB = 8
STEP = 32
MESH = pl.DeviceIdType.MESH


def split_chips(chips):
    inner = 1
    for size in range(1, chips + 1):
        if size * size <= chips and chips % size == 0:
            inner = size
    return chips // inner, inner


class Copies:
    def __init__(self, sems):
        self.sems = sems
        self.made = {}

    def start(self, k, src, dst, device):
        made = pltpu.make_async_remote_copy(
            src_ref=src,
            dst_ref=dst,
            send_sem=self.sems.at[0, k],
            recv_sem=self.sems.at[1, k],
            device_id=(device,),
            device_id_type=MESH,
        )
        made.start()
        self.made[k] = made

    def arrive(self):
        for made in self.made.values():
            made.wait_recv()

    def drain(self):
        for made in self.made.values():
            made.wait_send()


def kernel(
    outer, inner, cap, rows, cols,
    adv_id, slot_id, mask_hbm, adv_hbm, slot_hbm, limit_hbm, room_hbm, start_hbm, cost_hbm,
    primal_hbm, adv_out, slot_out,
    tile, price, blocks, adv_dual, slot_dual, limit, capacity, square, weight, row_part, col_sum, row_sum,
    half_adv, half_slot, totals, dual_buf, rest_buf, sums_one, sums_two, ids_buf,
    send_start, send_one, send_two, got_start, got_one, got_two,
    column_sems, plane_sems, in_sems, small_sems, out_sems,
):
    plane = 2 * inner
    me = lax.axis_index("tiles")
    p = lax.rem(me, plane)
    o = me // plane
    row_lines, col_lines = rows // LANES, cols // LANES
    groups = STEP // SUB
    mask_rows, mask_cols = mask_hbm.shape[2], mask_hbm.shape[1]

    small = [
        pltpu.make_async_copy(src, dst, small_sems.at[n])
        for n, (src, dst) in enumerate((
            (adv_hbm, adv_dual), (slot_hbm, slot_dual), (limit_hbm, limit), (room_hbm, capacity), (mask_hbm, blocks)))
    ]
    for made in small:
        made.start()
    loads = []
    for t in range(cap):
        pair = (
            pltpu.make_async_copy(start_hbm.at[t], tile.at[t], in_sems.at[0, t]),
            pltpu.make_async_copy(cost_hbm.at[t], price.at[t], in_sems.at[1, t]),
        )
        for made in pair:
            made.start()
        loads.append(pair)

    def in_column(k):
        return lax.rem(o + k, outer) * plane + p

    def in_plane(k):
        return o * plane + lax.rem(p + k, plane)

    barrier = pltpu.get_barrier_semaphore()
    peers = [in_column(k) for k in range(1, outer)] + [in_plane(k) for k in range(1, plane)]
    for peer in peers:
        pl.semaphore_signal(barrier, inc=1, device_id=(peer,), device_id_type=MESH)

    exchanges = [Copies(column_sems.at[g]) for g in range(4)] + [Copies(plane_sems.at[g]) for g in range(4)]
    duals, rest, first, second, named, part_start, part_one, part_two = exchanges

    def slot_at(e):
        return slice(e * col_lines, (e + 1) * col_lines)

    def adv_at(n, e):
        return slice(n * col_lines + e * row_lines, n * col_lines + (e + 1) * row_lines)

    id_line = col_lines + row_lines
    for t in range(cap):
        for n, ids in ((t, adv_id), (cap + t, slot_id)):
            value = jnp.full((1, LANES), ids[t].astype(jnp.float32))
            ids_buf[p, n:n + 1, :] = value
            rest_buf[o, id_line + n:id_line + n + 1, :] = value
    for made in small[:4]:
        made.wait()
    for r in range(row_lines):
        at = slice(r * LANES, (r + 1) * LANES)
        dual_buf[o, col_lines + r:col_lines + r + 1, :] = adv_dual[0:1, at]
        rest_buf[o, col_lines + r:col_lines + r + 1, :] = limit[0:1, at]
    for r in range(col_lines):
        at = slice(r * LANES, (r + 1) * LANES)
        dual_buf[o, r:r + 1, :] = slot_dual[0:1, at]
        rest_buf[o, r:r + 1, :] = capacity[0:1, at]

    def send_column(copies, buf):
        for k in range(outer - 1, 0, -1):
            copies.start(k, buf.at[o], buf.at[o], in_column(k))

    pl.semaphore_wait(barrier, len(peers))
    send_column(duals, dual_buf)
    for k in range(1, plane):
        named.start(k, ids_buf.at[p], ids_buf.at[p], in_plane(k))
    send_column(rest, rest_buf)

    small[4].wait()
    square[...] = jnp.zeros_like(square)
    for t in range(cap):
        alive = jnp.where(adv_id[t] >= 0, 1.0, 0.0).astype(jnp.float32)
        square[0:mask_cols, 0:mask_rows] = blocks[t].astype(jnp.float32) * alive
        turned = jnp.transpose(square[...])
        for j in range(mask_cols):
            weight[t, j] = jnp.broadcast_to(turned[0:mask_rows, j:j + 1], (mask_rows, LANES))

    def exists(t, at, j):
        return jnp.broadcast_to(weight[t, j, pl.ds(at, 1), :], (SUB, LANES))

    def sum_tile(t, value):
        def step(s, col):
            col = list(col)
            for g in range(groups):
                row = None
                for j in range(col_lines):
                    piece = value(s, g, j)
                    row = piece if row is None else row + piece
                    col[j] = col[j] + piece
                row_part[t, pl.ds(s * STEP + g * SUB, SUB), :] = row
            return tuple(col)

        zero = jnp.zeros((SUB, LANES), jnp.float32)
        return lax.fori_loop(0, rows // STEP, step, (zero,) * col_lines)

    def keep_cols(slot, t, col):
        for j in range(col_lines):
            col_sum[slot, t, j:j + 1, :] = jnp.sum(col[j], axis=0, keepdims=True)

    def keep_rows(slot):
        lane = lax.broadcasted_iota(jnp.int32, (LANES, LANES), 1)
        gathered = jnp.zeros((LANES, LANES), jnp.float32)
        for t in range(cap):
            for r in range(row_lines):
                sums = jnp.sum(row_part[t, r * LANES:(r + 1) * LANES, :], axis=1, keepdims=True)
                gathered = jnp.where(lane == t * row_lines + r, sums, gathered)
        row_sum[slot] = jnp.transpose(gathered)[0:cap * row_lines, :]

    def prepare(t):
        for made in loads[t]:
            made.wait()

        def step(s, col):
            col = list(col)
            for h in range(STEP // 16):
                row = [None, None]
                for j in range(col_lines):
                    at = (t, pl.ds(s * STEP + h * 16, 16), slice(j * LANES, (j + 1) * LANES))
                    x = tile[at]
                    tile[at] = x - 0.5 * price[at].astype(jnp.float32)
                    for half in range(2):
                        piece = x[half * SUB:(half + 1) * SUB] * exists(t, s * groups + h * 2 + half, j)
                        row[half] = piece if row[half] is None else row[half] + piece
                        col[j] = col[j] + piece
                for half in range(2):
                    row_part[t, pl.ds(s * STEP + h * 16 + half * SUB, SUB), :] = row[half]
            return tuple(col)

        zero = jnp.zeros((SUB, LANES), jnp.float32)
        keep_cols(0, t, lax.fori_loop(0, rows // STEP, step, (zero,) * col_lines))

    def less_price(t):
        def step(s, carry):
            for h in range(STEP // 16):
                for j in range(col_lines):
                    at = (t, pl.ds(s * STEP + h * 16, 16), slice(j * LANES, (j + 1) * LANES))
                    tile[at] = tile[at] - 0.5 * price[at].astype(jnp.float32)
            return carry

        lax.fori_loop(0, rows // STEP, step, 0)

    def set_duals(found):
        for t, (adv, slot) in enumerate(found):
            square[t * row_lines:(t + 1) * row_lines, :] = 0.5 * adv
            half_slot[t] = 0.5 * slot
        turned = jnp.transpose(square[...])
        for t in range(cap):
            for r in range(row_lines):
                at = t * row_lines + r
                half_adv[t, r * LANES:(r + 1) * LANES, :] = jnp.broadcast_to(turned[:, at:at + 1], (LANES, LANES))

    def update(t, slot):
        slots = [jnp.broadcast_to(half_slot[t, j:j + 1, :], (SUB, LANES)) for j in range(col_lines)]

        def value(s, g, j):
            at = (t, pl.ds(s * STEP + g * SUB, SUB), slice(j * LANES, (j + 1) * LANES))
            moved = tile[at] - half_adv[t, pl.ds(s * STEP + g * SUB, SUB), :] - slots[j]
            new = jnp.clip(moved, 0.0, 1.0) * exists(t, s * groups + g, j)
            tile[at] = new
            return new

        keep_cols(slot, t, sum_tile(t, value))

    def post(buf, slot):
        for t in range(cap):
            at = slice(t * row_lines, (t + 1) * row_lines)
            buf[o, slot_at(t), :] = 2.0 * col_sum[slot, t] - col_sum[slot - 1, t]
            buf[o, adv_at(cap, t), :] = 2.0 * row_sum[slot, at, :] - row_sum[slot - 1, at, :]

    def splat(value):
        return jnp.full((1, LANES), value.astype(jnp.float32))

    def tile_items(buf):
        return [
            (
                rest_buf[b, id_line + t:id_line + t + 1, :], rest_buf[b, id_line + cap + t:id_line + cap + t + 1, :],
                buf[b, adv_at(cap, t), :], buf[b, slot_at(t), :],
            )
            for b in range(outer) for t in range(cap)
        ]

    def block_items(buf, sign):
        return [
            (splat(b * plane + p), splat(b * plane + p), sign * buf[b, adv_at(1, 0), :], sign * buf[b, slot_at(0), :])
            for b in range(outer)
        ]

    def targets_of(q, own):
        found = []
        if own != "alone":
            found = [(ids_buf[q, t:t + 1, :], ids_buf[q, cap + t:cap + t + 1, :]) for t in range(cap)]
        if own:
            found.append((splat(o * plane + q),) * 2)
        return found

    def part(items, targets, into, add):
        n = len(targets)
        for e, (a, b) in enumerate(targets):
            adv = into[adv_at(n, e), :] if add else jnp.zeros((row_lines, LANES), jnp.float32)
            slot = into[slot_at(e), :] if add else jnp.zeros((col_lines, LANES), jnp.float32)
            for a_of, b_of, by_row, by_col in items:
                adv = adv + jnp.where(a_of == a, 1.0, 0.0) * by_row
                slot = slot + jnp.where(b_of == b, 1.0, 0.0) * by_col
            into[adv_at(n, e), :] = adv
            into[slot_at(e), :] = slot

    def parts(copies, items, own, send, got, add=False, go=True):
        order = list(range(plane - 1, -1, -1))
        for k in order:
            into = send.at[k] if k else got.at[0]
            part(items, targets_of(lax.rem(p + k, plane), own), into, add)
            if go and k:
                copies.start(k, send.at[k], got.at[k], in_plane(k))

    def total(got):
        value = got[0]
        for k in range(1, plane):
            value = value + got[k]
        return value

    prepare(0)
    named.arrive()
    duals.arrive()
    parts(part_start, block_items(dual_buf, 1.0), False, send_start, got_start)
    for t in range(1, cap):
        prepare(t)
    keep_rows(0)
    rest.arrive()
    part_start.arrive()

    old = total(got_start)
    set_duals([(old[adv_at(cap, t)], old[slot_at(t)]) for t in range(cap)])
    for t in range(cap):
        update(t, 1)
    keep_rows(1)
    post(sums_one, 1)
    send_column(first, sums_one)
    parts(part_one, block_items(rest_buf, -1.0), True, send_one, got_one, go=False)
    less_price(0)
    first.arrive()
    parts(part_one, tile_items(sums_one), True, send_one, got_one, add=True)
    for t in range(1, cap):
        less_price(t)
    part_one.arrive()

    moved = total(got_one)
    found = []
    for k in range(cap + 1):
        adv, slot = moved[adv_at(cap + 1, k)], moved[slot_at(k)]
        if k < cap:
            adv = jnp.maximum(old[adv_at(cap, k)] + adv / cols, 0.0)
            slot = jnp.maximum(old[slot_at(k)] + slot / rows, 0.0)
            found.append((adv, slot))
        else:
            totals[adv_at(1, 0), :] = jnp.maximum(dual_buf[o, adv_at(1, 0), :] + adv / cols, 0.0)
            totals[slot_at(0), :] = jnp.maximum(dual_buf[o, slot_at(0), :] + slot / rows, 0.0)

    set_duals(found)
    stores = []
    for t in range(cap):
        update(t, 2)
        made = pltpu.make_async_copy(tile.at[t], primal_hbm.at[t], out_sems.at[t])
        made.start()
        stores.append(made)
    keep_rows(2)
    post(sums_two, 2)
    send_column(second, sums_two)
    second.arrive()
    parts(part_two, tile_items(sums_two), "alone", send_two, got_two)
    part_two.arrive()

    use = total(got_two)
    adv = totals[adv_at(1, 0), :] + (use[adv_at(1, 0)] - rest_buf[o, adv_at(1, 0), :]) / cols
    slot = totals[slot_at(0), :] + (use[slot_at(0)] - rest_buf[o, slot_at(0), :]) / rows
    for r in range(row_lines):
        adv_out[0:1, r * LANES:(r + 1) * LANES] = jnp.maximum(adv[r:r + 1, :], 0.0)
    for r in range(col_lines):
        slot_out[0:1, r * LANES:(r + 1) * LANES] = jnp.maximum(slot[r:r + 1, :], 0.0)

    for copies in exchanges:
        copies.drain()
    for made in stores:
        made.wait()


def store(primal, adv, slot, primal_out, adv_out, slot_out, held, small, in_sems, out_sems):
    pieces = in_sems.shape[0] - len(small)
    cap, rows = primal.shape[:2]
    size = cap * rows // pieces
    routes = [(adv, small[0], adv_out), (slot, small[1], slot_out)]
    for n in range(pieces):
        at = (n * size // rows, pl.ds(n * size % rows, size))
        routes.append((primal.at[at], held.at[at], primal_out.at[at]))
    into = [pltpu.make_async_copy(src, mid, in_sems.at[n]) for n, (src, mid, _) in enumerate(routes)]
    out = [pltpu.make_async_copy(mid, dst, out_sems.at[n]) for n, (_, mid, dst) in enumerate(routes)]
    for copy in into:
        copy.start()
    for first, then in zip(into, out):
        first.wait()
        then.start()
    for copy in out:
        copy.wait()


def body(primal_start, cost, mask, tile_adv, tile_slot, adv_dual, slot_dual, spend_limit, capacity):
    devices = lax.axis_size("tiles")
    outer, inner = split_chips(devices // 2)
    plane = 2 * inner
    cap, rows, cols = primal_start.shape
    row_lines, col_lines = rows // LANES, cols // LANES
    entry = row_lines + col_lines
    f32 = jnp.float32
    vmem = pl.BlockSpec(memory_space=pltpu.VMEM)
    smem = pl.BlockSpec(memory_space=pltpu.SMEM)
    hbm = pl.BlockSpec(memory_space=pltpu.HBM)
    mask = jnp.swapaxes(mask, 1, 2)
    outs = (
        jax.ShapeDtypeStruct(primal_start.shape, f32),
        jax.ShapeDtypeStruct(adv_dual.shape, f32),
        jax.ShapeDtypeStruct(slot_dual.shape, f32),
    )
    results = pl.pallas_call(
        functools.partial(kernel, outer, inner, cap, rows, cols),
        out_shape=outs,
        in_specs=[smem, smem, hbm, hbm, hbm, hbm, hbm, hbm, hbm],
        out_specs=(hbm, vmem, vmem),
        scratch_shapes=[
            pltpu.VMEM((cap, rows, cols), f32),
            pltpu.VMEM((cap, rows, cols), cost.dtype),
            pltpu.VMEM(mask.shape, mask.dtype),
            pltpu.VMEM(adv_dual.shape, f32),
            pltpu.VMEM(slot_dual.shape, f32),
            pltpu.VMEM(spend_limit.shape, f32),
            pltpu.VMEM(capacity.shape, f32),
            pltpu.VMEM((LANES, LANES), f32),
            pltpu.VMEM((cap, mask.shape[1], mask.shape[2], LANES), f32),
            pltpu.VMEM((cap, rows, LANES), f32),
            pltpu.VMEM((ITERS + 1, cap, col_lines, LANES), f32),
            pltpu.VMEM((ITERS + 1, cap * row_lines, LANES), f32),
            pltpu.VMEM((cap, rows, LANES), f32),
            pltpu.VMEM((cap, col_lines, LANES), f32),
            pltpu.VMEM((entry, LANES), f32),
            pltpu.VMEM((outer, entry, LANES), f32),
            pltpu.VMEM((outer, entry + 2 * cap, LANES), f32),
            pltpu.VMEM((outer, cap * entry, LANES), f32),
            pltpu.VMEM((outer, cap * entry, LANES), f32),
            pltpu.VMEM((plane, 2 * cap, LANES), f32),
            pltpu.VMEM((plane, cap * entry, LANES), f32),
            pltpu.VMEM((plane, (cap + 1) * entry, LANES), f32),
            pltpu.VMEM((plane, entry, LANES), f32),
            pltpu.VMEM((plane, cap * entry, LANES), f32),
            pltpu.VMEM((plane, (cap + 1) * entry, LANES), f32),
            pltpu.VMEM((plane, entry, LANES), f32),
            pltpu.SemaphoreType.DMA((4, 2, outer)),
            pltpu.SemaphoreType.DMA((4, 2, plane)),
            pltpu.SemaphoreType.DMA((2, cap)),
            pltpu.SemaphoreType.DMA((5,)),
            pltpu.SemaphoreType.DMA((cap,)),
        ],
        compiler_params=pltpu.CompilerParams(
            collective_id=0, has_side_effects=True, vmem_limit_bytes=60 * 1024 * 1024
        ),
    )(tile_adv, tile_slot, mask, adv_dual, slot_dual, spend_limit, capacity, primal_start, cost)
    return pl.pallas_call(
        store,
        out_shape=outs,
        in_specs=[pl.BlockSpec(memory_space=pl.ANY)] * len(outs),
        out_specs=(hbm,) * len(outs),
        scratch_shapes=[
            pltpu.VMEM(primal_start.shape, f32),
            (pltpu.VMEM(adv_dual.shape, f32), pltpu.VMEM(slot_dual.shape, f32)),
            pltpu.SemaphoreType.DMA((4 * cap + 2,)),
            pltpu.SemaphoreType.DMA((4 * cap + 2,)),
        ],
        compiler_params=pltpu.CompilerParams(vmem_limit_bytes=60 * 1024 * 1024),
    )(*results)


def solution(mesh):
    return jax.shard_map(
        body,
        mesh=mesh,
        in_specs=(
            P("tiles", None, None),
            P("tiles", None, None),
            P("tiles", None, None),
            P("tiles"),
            P("tiles"),
            P("tiles", None),
            P("tiles", None),
            P("tiles", None),
            P("tiles", None),
        ),
        out_specs=(P("tiles", None, None), P("tiles", None), P("tiles", None)),
        check_vma=False,
    )
```

```python
import functools

import jax
import jax.numpy as jnp
from jax import lax
from jax.experimental import pallas as pl
from jax.experimental.pallas import tpu as pltpu
from jax.sharding import PartitionSpec as P

ITERS = 2
LANES = 128
SUB = 8
STEP = 32
MESH = pl.DeviceIdType.MESH


def split_chips(chips):
    inner = 1
    for size in range(1, chips + 1):
        if size * size <= chips and chips % size == 0:
            inner = size
    return chips // inner, inner


class Copies:
    def __init__(self, sems):
        self.sems = sems
        self.made = {}

    def start(self, k, src, dst, device):
        made = pltpu.make_async_remote_copy(
            src_ref=src,
            dst_ref=dst,
            send_sem=self.sems.at[0, k],
            recv_sem=self.sems.at[1, k],
            device_id=(device,),
            device_id_type=MESH,
        )
        made.start()
        self.made[k] = made

    def arrive(self):
        for made in self.made.values():
            made.wait_recv()

    def drain(self):
        for made in self.made.values():
            made.wait_send()


def kernel(
    outer, inner, cap, rows, cols,
    adv_id, slot_id, mask_hbm, adv_hbm, slot_hbm, limit_hbm, room_hbm, start_hbm, cost_hbm,
    primal_hbm, adv_out, slot_out,
    tile, price, blocks, adv_dual, slot_dual, limit, capacity, square, weight, row_part, col_sum, row_sum,
    half_adv, half_slot, totals, dual_buf, rest_buf, sums_one, sums_two, ids_buf,
    send_start, send_one, send_two, got_start, got_one, got_two,
    column_sems, plane_sems, in_sems, small_sems, out_sems,
):
    plane = 2 * inner
    me = lax.axis_index("tiles")
    p = lax.rem(me, plane)
    o = me // plane
    row_lines, col_lines = rows // LANES, cols // LANES
    groups = STEP // SUB
    mask_rows, mask_cols = mask_hbm.shape[2], mask_hbm.shape[1]

    def in_column(k):
        return lax.rem(o + k, outer) * plane + p

    def in_plane(k):
        return o * plane + lax.rem(p + k, plane)

    barrier = pltpu.get_barrier_semaphore()
    peers = [in_column(k) for k in range(1, outer)] + [in_plane(k) for k in range(1, plane)]
    for peer in peers:
        pl.semaphore_signal(barrier, inc=1, device_id=(peer,), device_id_type=MESH)

    small = [
        pltpu.make_async_copy(src, dst, small_sems.at[n])
        for n, (src, dst) in enumerate((
            (adv_hbm, adv_dual), (slot_hbm, slot_dual), (limit_hbm, limit), (room_hbm, capacity), (mask_hbm, blocks)))
    ]
    for made in small:
        made.start()
    loads = []
    for t in range(cap):
        pair = (
            pltpu.make_async_copy(start_hbm.at[t], tile.at[t], in_sems.at[0, t]),
            pltpu.make_async_copy(cost_hbm.at[t], price.at[t], in_sems.at[1, t]),
        )
        for made in pair:
            made.start()
        loads.append(pair)

    along = [Copies(column_sems.at[g]) for g in range(2 + 2 * cap)]
    across = [Copies(plane_sems.at[g]) for g in range(4)]
    duals, rest, first, second = along[0], along[1], along[2:2 + cap], along[2 + cap:]
    named, part_start, part_one, part_two = across

    def slot_at(e):
        return slice(e * col_lines, (e + 1) * col_lines)

    def adv_at(n, e):
        return slice(n * col_lines + e * row_lines, n * col_lines + (e + 1) * row_lines)

    id_line = col_lines + row_lines
    for t in range(cap):
        for n, ids in ((t, adv_id), (cap + t, slot_id)):
            value = jnp.full((1, LANES), ids[t].astype(jnp.float32))
            ids_buf[p, n:n + 1, :] = value
            rest_buf[o, id_line + n:id_line + n + 1, :] = value
    for made in small[:4]:
        made.wait()
    for r in range(row_lines):
        at = slice(r * LANES, (r + 1) * LANES)
        dual_buf[o, col_lines + r:col_lines + r + 1, :] = adv_dual[0:1, at]
        rest_buf[o, col_lines + r:col_lines + r + 1, :] = limit[0:1, at]
    for r in range(col_lines):
        at = slice(r * LANES, (r + 1) * LANES)
        dual_buf[o, r:r + 1, :] = slot_dual[0:1, at]
        rest_buf[o, r:r + 1, :] = capacity[0:1, at]

    def send_column(copies, buf):
        for k in range(outer - 1, 0, -1):
            copies.start(k, buf.at[o], buf.at[o], in_column(k))

    pl.semaphore_wait(barrier, len(peers))
    send_column(duals, dual_buf)
    for k in range(1, plane):
        named.start(k, ids_buf.at[p], ids_buf.at[p], in_plane(k))
    send_column(rest, rest_buf)

    small[4].wait()
    square[...] = jnp.zeros_like(square)
    for t in range(cap):
        alive = jnp.where(adv_id[t] >= 0, 1.0, 0.0).astype(jnp.float32)
        square[0:mask_cols, 0:mask_rows] = blocks[t].astype(jnp.float32) * alive
        turned = jnp.transpose(square[...])
        for j in range(mask_cols):
            weight[t, j] = jnp.broadcast_to(turned[0:mask_rows, j:j + 1], (mask_rows, LANES))

    def exists(t, at, j):
        return jnp.broadcast_to(weight[t, j, pl.ds(at, 1), :], (SUB, LANES))

    def sum_tile(t, value):
        def step(s, col):
            col = list(col)
            for g in range(groups):
                row = None
                for j in range(col_lines):
                    piece = value(s, g, j)
                    row = piece if row is None else row + piece
                    col[j] = col[j] + piece
                row_part[t, pl.ds(s * STEP + g * SUB, SUB), :] = row
            return tuple(col)

        zero = jnp.zeros((SUB, LANES), jnp.float32)
        return lax.fori_loop(0, rows // STEP, step, (zero,) * col_lines)

    def keep_cols(slot, t, col):
        for j in range(col_lines):
            col_sum[slot, t, j:j + 1, :] = jnp.sum(col[j], axis=0, keepdims=True)

    def keep_rows(slot, t):
        lane = lax.broadcasted_iota(jnp.int32, (LANES, LANES), 1)
        gathered = jnp.zeros((LANES, LANES), jnp.float32)
        for r in range(row_lines):
            sums = jnp.sum(row_part[t, r * LANES:(r + 1) * LANES, :], axis=1, keepdims=True)
            gathered = jnp.where(lane == r, sums, gathered)
        row_sum[slot, t] = jnp.transpose(gathered)[0:row_lines, :]

    def prepare(t):
        for made in loads[t]:
            made.wait()

        def step(s, col):
            col = list(col)
            for h in range(STEP // 16):
                row = [None, None]
                for j in range(col_lines):
                    at = (t, pl.ds(s * STEP + h * 16, 16), slice(j * LANES, (j + 1) * LANES))
                    x = tile[at]
                    tile[at] = x - 0.5 * price[at].astype(jnp.float32)
                    for half in range(2):
                        piece = x[half * SUB:(half + 1) * SUB] * exists(t, s * groups + h * 2 + half, j)
                        row[half] = piece if row[half] is None else row[half] + piece
                        col[j] = col[j] + piece
                for half in range(2):
                    row_part[t, pl.ds(s * STEP + h * 16 + half * SUB, SUB), :] = row[half]
            return tuple(col)

        zero = jnp.zeros((SUB, LANES), jnp.float32)
        keep_cols(0, t, lax.fori_loop(0, rows // STEP, step, (zero,) * col_lines))

    def less_price(t):
        def step(s, carry):
            for h in range(STEP // 16):
                for j in range(col_lines):
                    at = (t, pl.ds(s * STEP + h * 16, 16), slice(j * LANES, (j + 1) * LANES))
                    tile[at] = tile[at] - 0.5 * price[at].astype(jnp.float32)
            return carry

        lax.fori_loop(0, rows // STEP, step, 0)

    def set_duals(found):
        for t, (adv, slot) in enumerate(found):
            square[t * row_lines:(t + 1) * row_lines, :] = 0.5 * adv
            half_slot[t] = 0.5 * slot
        turned = jnp.transpose(square[...])
        for t in range(cap):
            for r in range(row_lines):
                at = t * row_lines + r
                half_adv[t, r * LANES:(r + 1) * LANES, :] = jnp.broadcast_to(turned[:, at:at + 1], (LANES, LANES))

    def update(t, slot):
        slots = [jnp.broadcast_to(half_slot[t, j:j + 1, :], (SUB, LANES)) for j in range(col_lines)]

        def value(s, g, j):
            at = (t, pl.ds(s * STEP + g * SUB, SUB), slice(j * LANES, (j + 1) * LANES))
            moved = tile[at] - half_adv[t, pl.ds(s * STEP + g * SUB, SUB), :] - slots[j]
            new = jnp.clip(moved, 0.0, 1.0) * exists(t, s * groups + g, j)
            tile[at] = new
            return new

        keep_cols(slot, t, sum_tile(t, value))

    def post(buf, slot, t):
        buf[t, o, slot_at(0), :] = 2.0 * col_sum[slot, t] - col_sum[slot - 1, t]
        buf[t, o, adv_at(1, 0), :] = 2.0 * row_sum[slot, t] - row_sum[slot - 1, t]

    def splat(value):
        return jnp.full((1, LANES), value.astype(jnp.float32))

    def tile_items(buf, t):
        return [
            (
                rest_buf[b, id_line + t:id_line + t + 1, :], rest_buf[b, id_line + cap + t:id_line + cap + t + 1, :],
                buf[t, b, adv_at(1, 0), :], buf[t, b, slot_at(0), :],
            )
            for b in range(outer)
        ]

    def block_items(buf, sign):
        return [
            (splat(b * plane + p), splat(b * plane + p), sign * buf[b, adv_at(1, 0), :], sign * buf[b, slot_at(0), :])
            for b in range(outer)
        ]

    def targets_of(q, own):
        found = []
        if own != "alone":
            found = [(ids_buf[q, t:t + 1, :], ids_buf[q, cap + t:cap + t + 1, :]) for t in range(cap)]
        if own:
            found.append((splat(o * plane + q),) * 2)
        return found

    def part(items, targets, into, add):
        n = len(targets)
        for e, (a, b) in enumerate(targets):
            adv = into[adv_at(n, e), :] if add else jnp.zeros((row_lines, LANES), jnp.float32)
            slot = into[slot_at(e), :] if add else jnp.zeros((col_lines, LANES), jnp.float32)
            for a_of, b_of, by_row, by_col in items:
                adv = adv + jnp.where(a_of == a, 1.0, 0.0) * by_row
                slot = slot + jnp.where(b_of == b, 1.0, 0.0) * by_col
            into[adv_at(n, e), :] = adv
            into[slot_at(e), :] = slot

    def parts(copies, items, own, send, got, add=False, go=True):
        order = list(range(plane - 1, -1, -1))
        for k in order:
            into = send.at[k] if k else got.at[0]
            part(items, targets_of(lax.rem(p + k, plane), own), into, add)
            if go and k:
                copies.start(k, send.at[k], got.at[k], in_plane(k))

    def total(got):
        value = got[0]
        for k in range(1, plane):
            value = value + got[k]
        return value

    named.arrive()
    duals.arrive()
    parts(part_start, block_items(dual_buf, 1.0), False, send_start, got_start)
    for t in range(cap):
        prepare(t)
        keep_rows(0, t)
    rest.arrive()
    part_start.arrive()

    old = total(got_start)
    set_duals([(old[adv_at(cap, t)], old[slot_at(t)]) for t in range(cap)])
    for t in range(cap):
        update(t, 1)
        keep_rows(1, t)
        post(sums_one, 1, t)
        send_column(first[t], sums_one.at[t])
    parts(part_one, block_items(rest_buf, -1.0), True, send_one, got_one, go=False)
    less_price(0)
    for t in range(cap):
        first[t].arrive()
        parts(part_one, tile_items(sums_one, t), True, send_one, got_one, add=True, go=t == cap - 1)
    for t in range(1, cap):
        less_price(t)
    part_one.arrive()

    moved = total(got_one)
    found = []
    for k in range(cap + 1):
        adv, slot = moved[adv_at(cap + 1, k)], moved[slot_at(k)]
        if k < cap:
            adv = jnp.maximum(old[adv_at(cap, k)] + adv / cols, 0.0)
            slot = jnp.maximum(old[slot_at(k)] + slot / rows, 0.0)
            found.append((adv, slot))
        else:
            totals[adv_at(1, 0), :] = jnp.maximum(dual_buf[o, adv_at(1, 0), :] + adv / cols, 0.0)
            totals[slot_at(0), :] = jnp.maximum(dual_buf[o, slot_at(0), :] + slot / rows, 0.0)

    set_duals(found)
    stores = []
    for t in range(cap):
        update(t, 2)
        made = pltpu.make_async_copy(tile.at[t], primal_hbm.at[t], out_sems.at[t])
        made.start()
        stores.append(made)
        keep_rows(2, t)
        post(sums_two, 2, t)
        send_column(second[t], sums_two.at[t])
    for t in range(cap):
        second[t].arrive()
        parts(part_two, tile_items(sums_two, t), "alone", send_two, got_two, add=t > 0, go=t == cap - 1)
    part_two.arrive()

    use = total(got_two)
    adv = totals[adv_at(1, 0), :] + (use[adv_at(1, 0)] - rest_buf[o, adv_at(1, 0), :]) / cols
    slot = totals[slot_at(0), :] + (use[slot_at(0)] - rest_buf[o, slot_at(0), :]) / rows
    for r in range(row_lines):
        adv_out[0:1, r * LANES:(r + 1) * LANES] = jnp.maximum(adv[r:r + 1, :], 0.0)
    for r in range(col_lines):
        slot_out[0:1, r * LANES:(r + 1) * LANES] = jnp.maximum(slot[r:r + 1, :], 0.0)

    for copies in along + across:
        copies.drain()
    for made in stores:
        made.wait()


def store(primal, adv, slot, primal_out, adv_out, slot_out, held, small, in_sems, out_sems):
    pieces = in_sems.shape[0] - len(small)
    cap, rows = primal.shape[:2]
    size = cap * rows // pieces
    routes = [(adv, small[0], adv_out), (slot, small[1], slot_out)]
    for n in range(pieces):
        at = (n * size // rows, pl.ds(n * size % rows, size))
        routes.append((primal.at[at], held.at[at], primal_out.at[at]))
    into = [pltpu.make_async_copy(src, mid, in_sems.at[n]) for n, (src, mid, _) in enumerate(routes)]
    out = [pltpu.make_async_copy(mid, dst, out_sems.at[n]) for n, (_, mid, dst) in enumerate(routes)]
    for copy in into:
        copy.start()
    for first, then in zip(into, out):
        first.wait()
        then.start()
    for copy in out:
        copy.wait()


def body(primal_start, cost, mask, tile_adv, tile_slot, adv_dual, slot_dual, spend_limit, capacity):
    devices = lax.axis_size("tiles")
    outer, inner = split_chips(devices // 2)
    plane = 2 * inner
    cap, rows, cols = primal_start.shape
    row_lines, col_lines = rows // LANES, cols // LANES
    entry = row_lines + col_lines
    f32 = jnp.float32
    vmem = pl.BlockSpec(memory_space=pltpu.VMEM)
    smem = pl.BlockSpec(memory_space=pltpu.SMEM)
    hbm = pl.BlockSpec(memory_space=pltpu.HBM)
    mask = jnp.swapaxes(mask, 1, 2)
    outs = (
        jax.ShapeDtypeStruct(primal_start.shape, f32),
        jax.ShapeDtypeStruct(adv_dual.shape, f32),
        jax.ShapeDtypeStruct(slot_dual.shape, f32),
    )
    results = pl.pallas_call(
        functools.partial(kernel, outer, inner, cap, rows, cols),
        out_shape=outs,
        in_specs=[smem, smem, hbm, hbm, hbm, hbm, hbm, hbm, hbm],
        out_specs=(hbm, vmem, vmem),
        scratch_shapes=[
            pltpu.VMEM((cap, rows, cols), f32),
            pltpu.VMEM((cap, rows, cols), cost.dtype),
            pltpu.VMEM(mask.shape, mask.dtype),
            pltpu.VMEM(adv_dual.shape, f32),
            pltpu.VMEM(slot_dual.shape, f32),
            pltpu.VMEM(spend_limit.shape, f32),
            pltpu.VMEM(capacity.shape, f32),
            pltpu.VMEM((LANES, LANES), f32),
            pltpu.VMEM((cap, mask.shape[1], mask.shape[2], LANES), f32),
            pltpu.VMEM((cap, rows, LANES), f32),
            pltpu.VMEM((ITERS + 1, cap, col_lines, LANES), f32),
            pltpu.VMEM((ITERS + 1, cap, row_lines, LANES), f32),
            pltpu.VMEM((cap, rows, LANES), f32),
            pltpu.VMEM((cap, col_lines, LANES), f32),
            pltpu.VMEM((entry, LANES), f32),
            pltpu.VMEM((outer, entry, LANES), f32),
            pltpu.VMEM((outer, entry + 2 * cap, LANES), f32),
            pltpu.VMEM((cap, outer, entry, LANES), f32),
            pltpu.VMEM((cap, outer, entry, LANES), f32),
            pltpu.VMEM((plane, 2 * cap, LANES), f32),
            pltpu.VMEM((plane, cap * entry, LANES), f32),
            pltpu.VMEM((plane, (cap + 1) * entry, LANES), f32),
            pltpu.VMEM((plane, entry, LANES), f32),
            pltpu.VMEM((plane, cap * entry, LANES), f32),
            pltpu.VMEM((plane, (cap + 1) * entry, LANES), f32),
            pltpu.VMEM((plane, entry, LANES), f32),
            pltpu.SemaphoreType.DMA((2 + 2 * cap, 2, outer)),
            pltpu.SemaphoreType.DMA((4, 2, plane)),
            pltpu.SemaphoreType.DMA((2, cap)),
            pltpu.SemaphoreType.DMA((5,)),
            pltpu.SemaphoreType.DMA((cap,)),
        ],
        compiler_params=pltpu.CompilerParams(
            collective_id=0, has_side_effects=True, vmem_limit_bytes=60 * 1024 * 1024
        ),
    )(tile_adv, tile_slot, mask, adv_dual, slot_dual, spend_limit, capacity, primal_start, cost)
    return pl.pallas_call(
        store,
        out_shape=outs,
        in_specs=[pl.BlockSpec(memory_space=pl.ANY)] * len(outs),
        out_specs=(hbm,) * len(outs),
        scratch_shapes=[
            pltpu.VMEM(primal_start.shape, f32),
            (pltpu.VMEM(adv_dual.shape, f32), pltpu.VMEM(slot_dual.shape, f32)),
            pltpu.SemaphoreType.DMA((4 * cap + 2,)),
            pltpu.SemaphoreType.DMA((4 * cap + 2,)),
        ],
        compiler_params=pltpu.CompilerParams(vmem_limit_bytes=60 * 1024 * 1024),
    )(*results)


def solution(mesh):
    return jax.shard_map(
        body,
        mesh=mesh,
        in_specs=(
            P("tiles", None, None),
            P("tiles", None, None),
            P("tiles", None, None),
            P("tiles"),
            P("tiles"),
            P("tiles", None),
            P("tiles", None),
            P("tiles", None),
            P("tiles", None),
        ),
        out_specs=(P("tiles", None, None), P("tiles", None), P("tiles", None)),
        check_vma=False,
    )
```

```python
import functools

import jax
import jax.numpy as jnp
from jax import lax
from jax.experimental import pallas as pl
from jax.experimental.pallas import tpu as pltpu
from jax.sharding import PartitionSpec as P

ITERS = 2
LANES = 128
SUB = 8
STEP = 64
MESH = pl.DeviceIdType.MESH


def split_chips(chips):
    inner = 1
    for size in range(1, chips + 1):
        if size * size <= chips and chips % size == 0:
            inner = size
    return chips // inner, inner


class Copies:
    def __init__(self, sems):
        self.sems = sems
        self.made = {}

    def start(self, k, src, dst, device):
        made = pltpu.make_async_remote_copy(
            src_ref=src,
            dst_ref=dst,
            send_sem=self.sems.at[0, k],
            recv_sem=self.sems.at[1, k],
            device_id=(device,),
            device_id_type=MESH,
        )
        made.start()
        self.made[k] = made

    def arrive(self):
        for made in self.made.values():
            made.wait_recv()

    def drain(self):
        for made in self.made.values():
            made.wait_send()


def kernel(
    outer, inner, cap, rows, cols,
    adv_id, slot_id, mask_hbm, adv_hbm, slot_hbm, limit_hbm, room_hbm, start_hbm, cost_hbm,
    primal_hbm, adv_out, slot_out,
    tile, price, blocks, adv_dual, slot_dual, limit, capacity, square, weight, row_part, col_sum, row_sum,
    half_adv, half_slot, totals, dual_buf, rest_buf, sums_one, sums_two, ids_buf,
    send_start, send_one, send_two, got_start, got_one, got_two,
    column_sems, plane_sems, in_sems, small_sems, out_sems,
):
    plane = 2 * inner
    me = lax.axis_index("tiles")
    p = lax.rem(me, plane)
    o = me // plane
    row_lines, col_lines = rows // LANES, cols // LANES
    groups = STEP // SUB
    mask_rows, mask_cols = mask_hbm.shape[2], mask_hbm.shape[1]

    small = [
        pltpu.make_async_copy(src, dst, small_sems.at[n])
        for n, (src, dst) in enumerate((
            (adv_hbm, adv_dual), (slot_hbm, slot_dual), (limit_hbm, limit), (room_hbm, capacity), (mask_hbm, blocks)))
    ]
    for made in small:
        made.start()
    loads = []
    for t in range(cap):
        pair = (
            pltpu.make_async_copy(start_hbm.at[t], tile.at[t], in_sems.at[0, t]),
            pltpu.make_async_copy(cost_hbm.at[t], price.at[t], in_sems.at[1, t]),
        )
        for made in pair:
            made.start()
        loads.append(pair)

    def in_column(k):
        return lax.rem(o + k, outer) * plane + p

    def in_plane(k):
        return o * plane + lax.rem(p + k, plane)

    barrier = pltpu.get_barrier_semaphore()
    peers = [in_column(k) for k in range(1, outer)] + [in_plane(k) for k in range(1, plane)]
    for peer in peers:
        pl.semaphore_signal(barrier, inc=1, device_id=(peer,), device_id_type=MESH)

    exchanges = [Copies(column_sems.at[g]) for g in range(4)] + [Copies(plane_sems.at[g]) for g in range(4)]
    duals, rest, first, second, named, part_start, part_one, part_two = exchanges

    def slot_at(e):
        return slice(e * col_lines, (e + 1) * col_lines)

    def adv_at(n, e):
        return slice(n * col_lines + e * row_lines, n * col_lines + (e + 1) * row_lines)

    id_line = col_lines + row_lines
    for t in range(cap):
        for n, ids in ((t, adv_id), (cap + t, slot_id)):
            value = jnp.full((1, LANES), ids[t].astype(jnp.float32))
            ids_buf[p, n:n + 1, :] = value
            rest_buf[o, id_line + n:id_line + n + 1, :] = value
    for made in small[:4]:
        made.wait()
    for r in range(row_lines):
        at = slice(r * LANES, (r + 1) * LANES)
        dual_buf[o, col_lines + r:col_lines + r + 1, :] = adv_dual[0:1, at]
        rest_buf[o, col_lines + r:col_lines + r + 1, :] = limit[0:1, at]
    for r in range(col_lines):
        at = slice(r * LANES, (r + 1) * LANES)
        dual_buf[o, r:r + 1, :] = slot_dual[0:1, at]
        rest_buf[o, r:r + 1, :] = capacity[0:1, at]

    def send_column(copies, buf):
        for k in range(outer - 1, 0, -1):
            copies.start(k, buf.at[o], buf.at[o], in_column(k))

    pl.semaphore_wait(barrier, len(peers))
    send_column(duals, dual_buf)
    for k in range(1, plane):
        named.start(k, ids_buf.at[p], ids_buf.at[p], in_plane(k))
    send_column(rest, rest_buf)

    small[4].wait()
    square[...] = jnp.zeros_like(square)
    for t in range(cap):
        alive = jnp.where(adv_id[t] >= 0, 1.0, 0.0).astype(jnp.float32)
        square[0:mask_cols, 0:mask_rows] = blocks[t].astype(jnp.float32) * alive
        turned = jnp.transpose(square[...])
        for j in range(mask_cols):
            weight[t, j] = jnp.broadcast_to(turned[0:mask_rows, j:j + 1], (mask_rows, LANES))

    def exists(t, at, j):
        return jnp.broadcast_to(weight[t, j, pl.ds(at, 1), :], (SUB, LANES))

    def sum_tile(t, value):
        def step(s, col):
            col = list(col)
            for g in range(groups):
                row = None
                for j in range(col_lines):
                    piece = value(s, g, j)
                    row = piece if row is None else row + piece
                    col[j] = col[j] + piece
                row_part[t, pl.ds(s * STEP + g * SUB, SUB), :] = row
            return tuple(col)

        zero = jnp.zeros((SUB, LANES), jnp.float32)
        return lax.fori_loop(0, rows // STEP, step, (zero,) * col_lines)

    def keep_cols(slot, t, col):
        for j in range(col_lines):
            col_sum[slot, t, j:j + 1, :] = jnp.sum(col[j], axis=0, keepdims=True)

    def keep_rows(slot):
        lane = lax.broadcasted_iota(jnp.int32, (LANES, LANES), 1)
        gathered = jnp.zeros((LANES, LANES), jnp.float32)
        for t in range(cap):
            for r in range(row_lines):
                sums = jnp.sum(row_part[t, r * LANES:(r + 1) * LANES, :], axis=1, keepdims=True)
                gathered = jnp.where(lane == t * row_lines + r, sums, gathered)
        row_sum[slot] = jnp.transpose(gathered)[0:cap * row_lines, :]

    def prepare(t):
        for made in loads[t]:
            made.wait()

        def step(s, col):
            col = list(col)
            for h in range(STEP // 16):
                row = [None, None]
                for j in range(col_lines):
                    at = (t, pl.ds(s * STEP + h * 16, 16), slice(j * LANES, (j + 1) * LANES))
                    x = tile[at]
                    tile[at] = x - 0.5 * price[at].astype(jnp.float32)
                    for half in range(2):
                        piece = x[half * SUB:(half + 1) * SUB] * exists(t, s * groups + h * 2 + half, j)
                        row[half] = piece if row[half] is None else row[half] + piece
                        col[j] = col[j] + piece
                for half in range(2):
                    row_part[t, pl.ds(s * STEP + h * 16 + half * SUB, SUB), :] = row[half]
            return tuple(col)

        zero = jnp.zeros((SUB, LANES), jnp.float32)
        keep_cols(0, t, lax.fori_loop(0, rows // STEP, step, (zero,) * col_lines))

    def less_price(t):
        def step(s, carry):
            for h in range(STEP // 16):
                for j in range(col_lines):
                    at = (t, pl.ds(s * STEP + h * 16, 16), slice(j * LANES, (j + 1) * LANES))
                    tile[at] = tile[at] - 0.5 * price[at].astype(jnp.float32)
            return carry

        lax.fori_loop(0, rows // STEP, step, 0)

    def set_duals(found):
        for t, (adv, slot) in enumerate(found):
            square[t * row_lines:(t + 1) * row_lines, :] = 0.5 * adv
            half_slot[t] = 0.5 * slot
        turned = jnp.transpose(square[...])
        for t in range(cap):
            for r in range(row_lines):
                at = t * row_lines + r
                half_adv[t, r * LANES:(r + 1) * LANES, :] = jnp.broadcast_to(turned[:, at:at + 1], (LANES, LANES))

    def update(t, slot):
        slots = [jnp.broadcast_to(half_slot[t, j:j + 1, :], (SUB, LANES)) for j in range(col_lines)]

        def value(s, g, j):
            at = (t, pl.ds(s * STEP + g * SUB, SUB), slice(j * LANES, (j + 1) * LANES))
            moved = tile[at] - half_adv[t, pl.ds(s * STEP + g * SUB, SUB), :] - slots[j]
            new = jnp.clip(moved, 0.0, 1.0) * exists(t, s * groups + g, j)
            tile[at] = new
            return new

        keep_cols(slot, t, sum_tile(t, value))

    def post(buf, slot):
        for t in range(cap):
            at = slice(t * row_lines, (t + 1) * row_lines)
            buf[o, slot_at(t), :] = 2.0 * col_sum[slot, t] - col_sum[slot - 1, t]
            buf[o, adv_at(cap, t), :] = 2.0 * row_sum[slot, at, :] - row_sum[slot - 1, at, :]

    def wide(line, lines):
        return jnp.broadcast_to(line, (lines, LANES))

    def splat(value):
        return jnp.full((1, LANES), value.astype(jnp.float32))

    def tile_items(buf):
        return [
            (
                rest_buf[b, id_line + t:id_line + t + 1, :], rest_buf[b, id_line + cap + t:id_line + cap + t + 1, :],
                buf[b, adv_at(cap, t), :], buf[b, slot_at(t), :],
            )
            for b in range(outer) for t in range(cap)
        ]

    def block_items(buf, sign):
        return [
            (splat(b * plane + p), splat(b * plane + p), sign * buf[b, adv_at(1, 0), :], sign * buf[b, slot_at(0), :])
            for b in range(outer)
        ]

    def targets_of(q, own):
        found = []
        if own != "alone":
            found = [(ids_buf[q, t:t + 1, :], ids_buf[q, cap + t:cap + t + 1, :]) for t in range(cap)]
        if own:
            found.append((splat(o * plane + q),) * 2)
        return found

    def part(items, targets, into, add):
        n = len(targets)
        for e, (a, b) in enumerate(targets):
            adv = into[adv_at(n, e), :] if add else jnp.zeros((row_lines, LANES), jnp.float32)
            slot = into[slot_at(e), :] if add else jnp.zeros((col_lines, LANES), jnp.float32)
            for a_of, b_of, by_row, by_col in items:
                adv = adv + jnp.where(wide(a_of, row_lines) == wide(a, row_lines), by_row, 0.0)
                slot = slot + jnp.where(wide(b_of, col_lines) == wide(b, col_lines), by_col, 0.0)
            into[adv_at(n, e), :] = adv
            into[slot_at(e), :] = slot

    def parts(copies, items, own, send, got, add=False, go=True):
        order = list(range(plane - 1, -1, -1))
        for k in order:
            into = send.at[k] if k else got.at[0]
            part(items, targets_of(lax.rem(p + k, plane), own), into, add)
            if go and k:
                copies.start(k, send.at[k], got.at[k], in_plane(k))

    def total(got):
        value = got[0]
        for k in range(1, plane):
            value = value + got[k]
        return value

    named.arrive()
    duals.arrive()
    parts(part_start, block_items(dual_buf, 1.0), False, send_start, got_start)
    for t in range(cap):
        prepare(t)
    keep_rows(0)
    rest.arrive()
    part_start.arrive()

    old = total(got_start)
    set_duals([(old[adv_at(cap, t)], old[slot_at(t)]) for t in range(cap)])
    for t in range(cap):
        update(t, 1)
    keep_rows(1)
    post(sums_one, 1)
    send_column(first, sums_one)
    parts(part_one, block_items(rest_buf, -1.0), True, send_one, got_one, go=False)
    less_price(0)
    first.arrive()
    parts(part_one, tile_items(sums_one), True, send_one, got_one, add=True)
    for t in range(1, cap):
        less_price(t)
    part_one.arrive()

    moved = total(got_one)
    found = []
    for k in range(cap + 1):
        adv, slot = moved[adv_at(cap + 1, k)], moved[slot_at(k)]
        if k < cap:
            adv = jnp.maximum(old[adv_at(cap, k)] + adv / cols, 0.0)
            slot = jnp.maximum(old[slot_at(k)] + slot / rows, 0.0)
            found.append((adv, slot))
        else:
            totals[adv_at(1, 0), :] = jnp.maximum(dual_buf[o, adv_at(1, 0), :] + adv / cols, 0.0)
            totals[slot_at(0), :] = jnp.maximum(dual_buf[o, slot_at(0), :] + slot / rows, 0.0)

    set_duals(found)
    stores = []
    for t in range(cap):
        update(t, 2)
        made = pltpu.make_async_copy(tile.at[t], primal_hbm.at[t], out_sems.at[t])
        made.start()
        stores.append(made)
    keep_rows(2)
    post(sums_two, 2)
    send_column(second, sums_two)
    second.arrive()
    parts(part_two, tile_items(sums_two), "alone", send_two, got_two)
    part_two.arrive()

    use = total(got_two)
    adv = totals[adv_at(1, 0), :] + (use[adv_at(1, 0)] - rest_buf[o, adv_at(1, 0), :]) / cols
    slot = totals[slot_at(0), :] + (use[slot_at(0)] - rest_buf[o, slot_at(0), :]) / rows
    for r in range(row_lines):
        adv_out[0:1, r * LANES:(r + 1) * LANES] = jnp.maximum(adv[r:r + 1, :], 0.0)
    for r in range(col_lines):
        slot_out[0:1, r * LANES:(r + 1) * LANES] = jnp.maximum(slot[r:r + 1, :], 0.0)

    for copies in exchanges:
        copies.drain()
    for made in stores:
        made.wait()


def store(primal, adv, slot, primal_out, adv_out, slot_out, held, small, in_sems, out_sems):
    pieces = in_sems.shape[0] - len(small)
    cap, rows = primal.shape[:2]
    size = cap * rows // pieces
    routes = [(adv, small[0], adv_out), (slot, small[1], slot_out)]
    for n in range(pieces):
        at = (n * size // rows, pl.ds(n * size % rows, size))
        routes.append((primal.at[at], held.at[at], primal_out.at[at]))
    into = [pltpu.make_async_copy(src, mid, in_sems.at[n]) for n, (src, mid, _) in enumerate(routes)]
    out = [pltpu.make_async_copy(mid, dst, out_sems.at[n]) for n, (_, mid, dst) in enumerate(routes)]
    for copy in into:
        copy.start()
    for first, then in zip(into, out):
        first.wait()
        then.start()
    for copy in out:
        copy.wait()


def body(primal_start, cost, mask, tile_adv, tile_slot, adv_dual, slot_dual, spend_limit, capacity):
    devices = lax.axis_size("tiles")
    outer, inner = split_chips(devices // 2)
    plane = 2 * inner
    cap, rows, cols = primal_start.shape
    row_lines, col_lines = rows // LANES, cols // LANES
    entry = row_lines + col_lines
    f32 = jnp.float32
    vmem = pl.BlockSpec(memory_space=pltpu.VMEM)
    smem = pl.BlockSpec(memory_space=pltpu.SMEM)
    hbm = pl.BlockSpec(memory_space=pltpu.HBM)
    mask = jnp.swapaxes(mask, 1, 2)
    outs = (
        jax.ShapeDtypeStruct(primal_start.shape, f32),
        jax.ShapeDtypeStruct(adv_dual.shape, f32),
        jax.ShapeDtypeStruct(slot_dual.shape, f32),
    )
    results = pl.pallas_call(
        functools.partial(kernel, outer, inner, cap, rows, cols),
        out_shape=outs,
        in_specs=[smem, smem, hbm, hbm, hbm, hbm, hbm, hbm, hbm],
        out_specs=(hbm, vmem, vmem),
        scratch_shapes=[
            pltpu.VMEM((cap, rows, cols), f32),
            pltpu.VMEM((cap, rows, cols), cost.dtype),
            pltpu.VMEM(mask.shape, mask.dtype),
            pltpu.VMEM(adv_dual.shape, f32),
            pltpu.VMEM(slot_dual.shape, f32),
            pltpu.VMEM(spend_limit.shape, f32),
            pltpu.VMEM(capacity.shape, f32),
            pltpu.VMEM((LANES, LANES), f32),
            pltpu.VMEM((cap, mask.shape[1], mask.shape[2], LANES), f32),
            pltpu.VMEM((cap, rows, LANES), f32),
            pltpu.VMEM((ITERS + 1, cap, col_lines, LANES), f32),
            pltpu.VMEM((ITERS + 1, cap * row_lines, LANES), f32),
            pltpu.VMEM((cap, rows, LANES), f32),
            pltpu.VMEM((cap, col_lines, LANES), f32),
            pltpu.VMEM((entry, LANES), f32),
            pltpu.VMEM((outer, entry, LANES), f32),
            pltpu.VMEM((outer, entry + 2 * cap, LANES), f32),
            pltpu.VMEM((outer, cap * entry, LANES), f32),
            pltpu.VMEM((outer, cap * entry, LANES), f32),
            pltpu.VMEM((plane, 2 * cap, LANES), f32),
            pltpu.VMEM((plane, cap * entry, LANES), f32),
            pltpu.VMEM((plane, (cap + 1) * entry, LANES), f32),
            pltpu.VMEM((plane, entry, LANES), f32),
            pltpu.VMEM((plane, cap * entry, LANES), f32),
            pltpu.VMEM((plane, (cap + 1) * entry, LANES), f32),
            pltpu.VMEM((plane, entry, LANES), f32),
            pltpu.SemaphoreType.DMA((4, 2, outer)),
            pltpu.SemaphoreType.DMA((4, 2, plane)),
            pltpu.SemaphoreType.DMA((2, cap)),
            pltpu.SemaphoreType.DMA((5,)),
            pltpu.SemaphoreType.DMA((cap,)),
        ],
        compiler_params=pltpu.CompilerParams(
            collective_id=0, has_side_effects=True, vmem_limit_bytes=60 * 1024 * 1024
        ),
    )(tile_adv, tile_slot, mask, adv_dual, slot_dual, spend_limit, capacity, primal_start, cost)
    return pl.pallas_call(
        store,
        out_shape=outs,
        in_specs=[pl.BlockSpec(memory_space=pl.ANY)] * len(outs),
        out_specs=(hbm,) * len(outs),
        scratch_shapes=[
            pltpu.VMEM(primal_start.shape, f32),
            (pltpu.VMEM(adv_dual.shape, f32), pltpu.VMEM(slot_dual.shape, f32)),
            pltpu.SemaphoreType.DMA((4 * cap + 2,)),
            pltpu.SemaphoreType.DMA((4 * cap + 2,)),
        ],
        compiler_params=pltpu.CompilerParams(vmem_limit_bytes=60 * 1024 * 1024),
    )(*results)


def solution(mesh):
    return jax.shard_map(
        body,
        mesh=mesh,
        in_specs=(
            P("tiles", None, None),
            P("tiles", None, None),
            P("tiles", None, None),
            P("tiles"),
            P("tiles"),
            P("tiles", None),
            P("tiles", None),
            P("tiles", None),
            P("tiles", None),
        ),
        out_specs=(P("tiles", None, None), P("tiles", None), P("tiles", None)),
        check_vma=False,
    )
```
